768 devices in a mesh: gx: 12 (over z), gy: 64 (over x, y, core).
Axes of the slice: x: 4, y: 8, z: 12, core: 2. Of those that a mesh axis runs over, the one named last changes fastest.
Arguments:
- diffusivity: float32 [50, 512, 1536], P(None, 'gy', 'gx'), may hold values from 0.02 to 0.125
- land_mask: int32 [512, 1536], P('gy', 'gx'), may hold values 0 or 1
- innovation: float32 [50, 98304], P(None, ('gx', 'gy')), may hold values from -6 to 6
- inverse_variance: float32 [50, 98304], P(None, ('gx', 'gy')), may hold values from 0.5 to 4
- owner_ids: int32 [98304, 1], P(('gx', 'gy')), may hold values from 0 to 63; in each aligned block of 128 rows (0 to 127, 128 to 255, ...) at most 4 rows name the same one
- cell_index: int32 [768, 256], P(('gx', 'gy')), may hold values from 0 to 888
- corner_weights: float32 [4, 768, 256], P(None, ('gx', 'gy'))
Outputs:
- control: float32 [50, 512, 1536], P(None, 'gy', 'gx')
- residual: float32 [50, 512, 1536], P(None, 'gy', 'gx')
The draws below stay inside these ranges and needn't reach their ends.
Inputs may be any that keep to these rules, and one draw needn't show every extreme that they name: `owner_ids`: among the records of one device no tile index is named more than 4 times, and one is named exactly 4 times.
All inputs are finite; a program needn't handle non-finite values. No bound on the sum of `land_mask` on one device may be relied on, other than what follows from the above.
Results may differ from the reference program's by a relative error of at most 0.012.
Values sent between devices are 32-bit elements; how exact they have to be, the bound alone decides.
No kernel may reach another device: no remote copies, remote signals or barrier semaphores. Data moves between devices by JAX's collectives and lax.ppermute only.
A program may use at most 32 MiB of HBM per device.

```python
import math
import jax
import jax.numpy as jnp
import numpy as np
from jax import lax

CHAN = 50
CY = 8
CX = 128
CAP = 4
STEPS = 5
ITERS = 2
NY = 512
NX = 1536
DEVS = 768
SLOTS = 256
NOBS_DEV = 128
RECS = 98304
N_GX = 12
N_GY = 64


def draw_corner_weights(key, part):
    rows = N_GX * N_GY
    shape = (4, rows, N_GY * CAP)
    ramp = 1.0 + 2.0 * jnp.arange(rows, dtype=jnp.float32) / max(rows - 1, 1)
    base = jax.random.uniform(key, shape, jnp.float32, 0.05, 1.0)
    return base * ramp[None, :, None]


def with_ends(drawn, own_key, low, top_value):
    longest = drawn.shape.index(max(drawn.shape))
    spots = []
    for shift in (0, 1):
        where = [jax.random.randint(jax.random.fold_in(own_key, axis), (), 0, length) for axis, length in enumerate(drawn.shape)]
        where[longest] = (where[longest] + shift) % drawn.shape[longest]
        spots.append(tuple(where))
    return drawn.at[spots[0]].set(low).at[spots[1]].set(top_value)


def level_of(stream_key, shape, cuts, smallest, largest):
    loudness, own = 1.0, jax.random.fold_in(stream_key, 6)
    for dim, shards_of in cuts:
        draws = jnp.exp(jax.random.uniform(jax.random.fold_in(own, dim), (shards_of,), jnp.float32, smallest / len(cuts), largest / len(cuts)))
        loudness = loudness * jnp.repeat(draws, shape[dim] // shards_of).reshape([-1 if axis == dim else 1 for axis in range(len(shape))])
    return loudness


def routed_block(stream_key, own, number, rows, count, top, reach, lean):
    ranking = jax.random.permutation(stream_key, count)
    heavy_load, usual = load_shares(count, rows * top, reach, lean, True), load_shares(count, rows * top, reach, lean, False)
    places = jnp.arange(count)

    def named(sizes, turn):
        used = int((sizes > 0).sum())
        fixed = max(1, used // 4)
        moved = fixed + (places - fixed + turn * (used - fixed)) % max(1, count - fixed)
        return jnp.zeros((count,), jnp.int32).at[ranking[jnp.where(places < fixed, places, moved)]].set(jnp.asarray(sizes, jnp.int32))

    sizes = jnp.where(number % 4 == 0, named(heavy_load, number // 4), named(usual, number - number // 4 - 1))
    mixed = jax.random.permutation(jax.random.fold_in(own, 3), count)
    giver, taker = mixed[0:count // 2 * 2:2], mixed[1:count // 2 * 2:2]
    slack = jnp.minimum(sizes[giver] - 1, reach - sizes[taker]) // 2
    slack = jnp.where((giver == ranking[0]) | (taker == ranking[0]) | (sizes[taker] == 0), 0, jnp.maximum(slack, 0))
    moved = jax.random.randint(jax.random.fold_in(own, 4), (count // 2,), 0, 1 << 20) % (slack + 1)
    sizes = sizes.at[giver].add(-moved).at[taker].add(moved)
    items = jnp.searchsorted(jnp.cumsum(sizes), jnp.arange(rows * top), side="right").astype(jnp.int32)
    listing = items.reshape(top, rows).T
    listing = listing[jax.random.permutation(jax.random.fold_in(own, 1), rows)]
    turn = jax.random.randint(jax.random.fold_in(own, 2), (rows, 1), 0, top)
    return jnp.take_along_axis(listing, (jnp.arange(top)[None, :] + turn) % top, axis=1)


def load_shares(count, total, most, skew, full):
    portions = [(1 << 20) // math.isqrt(grade ** skew) + 1 for grade in range(1, count + 1)]
    largest = most if full else min(most, max(-(-total // count), total * portions[0] // sum(portions)))
    least = 1 if total - largest >= count - 1 else 0
    counts, rest = [largest] + [least] * (count - 1), total - largest - least * (count - 1)
    while rest > 0:
        candidates = [i for i in range(1, count) if counts[i] < largest] or [i for i in range(1, count) if counts[i] < most]
        whole, remaining = sum([portions[i] for i in candidates]), rest
        for i in candidates:
            addition = min(most - counts[i], max(1, remaining * portions[i] // whole), rest)
            counts[i] = counts[i] + addition
            rest = rest - addition
    return np.array(counts)


def scatter_about(rng, dims, scale, bound, cuts=(), kind=jnp.bfloat16):
    gain = level_of(rng, dims, cuts, -0.22, 0.18) if cuts else 1.0
    entries = jax.random.normal(rng, dims, jnp.float32) * scale * gain
    return jnp.minimum(jnp.maximum(entries, -bound), bound).astype(kind)


def setup_inputs(seed: int = 0) -> dict:
    streams_of = jax.random.split(jax.random.key(seed), 8)
    diffusivity = jnp.clip(jnp.exp(math.log(0.125) - 1.8325815 * jax.random.uniform(streams_of[0], (CHAN, NY, NX), jnp.float32) ** level_of(streams_of[0], (CHAN, NY, NX), ((1, 64), (2, 12)), -0.2, 0.2)), 0.02, 0.125)
    land_mask = with_ends((jax.random.randint(streams_of[1], (NY, NX), 0, 5) < 4).astype(jnp.int32), jax.random.fold_in(streams_of[1], 1), 0, 1)
    innovation = scatter_about(streams_of[2], (CHAN, RECS), 1.0, 6.0, ((1, 768),), jnp.float32)
    inverse_variance = jnp.clip(jnp.exp(math.log(4.0) - 2.0794415 * jax.random.uniform(streams_of[3], (CHAN, RECS), jnp.float32) ** level_of(streams_of[3], (CHAN, RECS), ((1, 768),), -0.2, 0.2)), 0.5, 4.0)
    owner_ids_keys = jax.random.split(jax.random.fold_in(streams_of[4], 1), RECS // NOBS_DEV)
    owner_ids_turns = jax.random.permutation(jax.random.fold_in(streams_of[4], 3), RECS // NOBS_DEV)
    owner_ids = jax.vmap(lambda own, number: routed_block(jax.random.fold_in(streams_of[4], 2), own, number, NOBS_DEV, N_GY, 1, CAP, 2))(owner_ids_keys, owner_ids_turns).reshape((RECS, 1))
    cell_index = with_ends(jax.random.randint(streams_of[5], (DEVS, SLOTS), 0, (CY - 1) * (CX - 1)), jax.random.fold_in(streams_of[5], 1), 0, ((CY - 1) * (CX - 1)) - 1).astype(jnp.int32)
    corner_weights = draw_corner_weights(jax.random.fold_in(streams_of[7], 71), 0)
    return dict(diffusivity=diffusivity, land_mask=land_mask, innovation=innovation, inverse_variance=inverse_variance, owner_ids=owner_ids, cell_index=cell_index, corner_weights=corner_weights)


def smooth(field, sroot, ocean):
    field = ocean * field
    zero_row = jnp.zeros_like(field[:, :1])
    for step in range(STEPS):
        scaled = sroot * field
        north = jnp.concatenate([scaled[:, 1:], zero_row], axis=1)
        south = jnp.concatenate([zero_row, scaled[:, :-1]], axis=1)
        east = jnp.roll(scaled, -1, axis=2)
        west = jnp.roll(scaled, 1, axis=2)
        field = ocean * (field + sroot * (north + south + east + west - 4.0 * scaled))
    return field

def corner_table(cell_index):
    devs = cell_index.shape[0]
    width = CX * N_GX
    device = jnp.arange(devs, dtype=jnp.int32)[:, None]
    column = device // N_GY
    row = device % N_GY
    cell_row = cell_index // (CX - 1)
    cell_col = cell_index % (CX - 1)
    base = ((row * CY + cell_row) * width + column * CX + cell_col).reshape(-1)
    return jnp.stack([base, base + 1, base + width, base + width + 1]).astype(jnp.int32)

def sample(field, cells, weights):
    flat = field.reshape(field.shape[0], -1)
    total = weights[0][None, :] * jnp.take(flat, cells[0], axis=1)
    for corner in range(1, 4):
        total = total + weights[corner][None, :] * jnp.take(flat, cells[corner], axis=1)
    return total

def spread(misfit, cells, weights, like):
    flat = jnp.zeros((like.shape[0], like.shape[1] * like.shape[2]), jnp.float32)
    terms = (weights[:, None, :] * misfit[None, :, :]).transpose(1, 0, 2).reshape(misfit.shape[0], -1)
    flat = flat.at[:, cells.reshape(-1)].add(terms)
    return flat.reshape(like.shape)

def slot_table(owner_ids):
    devs = N_GX * N_GY
    owner = owner_ids[:, 0].reshape(devs, -1)
    onehot = (owner[:, :, None] == jnp.arange(N_GY, dtype=jnp.int32)[None, None, :]).astype(jnp.int32)
    rank = lax.optimization_barrier(jnp.sum((jnp.cumsum(onehot, axis=1) - 1) * onehot, axis=2))
    device = jnp.arange(devs, dtype=jnp.int32)[:, None]
    tile = device // N_GY * N_GY + owner
    position = device % N_GY * CAP + rank
    return (tile * (N_GY * CAP) + position).reshape(-1).astype(jnp.int32)

def reference(diffusivity, land_mask, innovation, inverse_variance, owner_ids, cell_index, corner_weights):
    ocean = land_mask.astype(jnp.float32)[None, :, :]
    sroot = jnp.sqrt(diffusivity)
    slot = slot_table(owner_ids)
    total_slots = N_GX * N_GY * N_GY * CAP
    chan = innovation.shape[0]
    weight_slots = jnp.zeros((chan, total_slots), jnp.float32).at[:, slot].set(inverse_variance)
    target_slots = jnp.zeros((chan, total_slots), jnp.float32).at[:, slot].set(inverse_variance * innovation)
    cells = corner_table(cell_index)
    weights = corner_weights.reshape(4, -1)

    def hessian(direction):
        state = smooth(direction, sroot, ocean)
        misfit = weight_slots * sample(state, cells, weights)
        return direction + smooth(spread(misfit, cells, weights, direction), sroot, ocean)
    rhs = smooth(spread(target_slots, cells, weights, diffusivity), sroot, ocean)
    control = jnp.zeros_like(rhs)
    residual = rhs
    direction = rhs
    norm_now = jnp.sum(residual * residual)
    for step in range(ITERS):
        image = hessian(direction)
        alpha = norm_now / jnp.sum(direction * image)
        control = control + alpha * direction
        residual = residual - alpha * image
        norm_next = jnp.sum(residual * residual)
        direction = residual + norm_next / norm_now * direction
        norm_now = norm_next
    return (control, residual)
```

```python
import functools

import jax
import jax.numpy as jnp
from jax import lax
from jax.experimental import pallas as pl
from jax.experimental.pallas import tpu as pltpu
from jax.sharding import PartitionSpec as P

CAP = 4
STEPS = 5
CHAN = 50
WIN = 32
LOW = 24
FULL = 56
COLS = 128
CY = 8
ROWS = 2 * CY
FAR = 2 * STEPS


def call(body, outs, flops, scratch=(), scalars=0):
    def run(*args):
        size = sum(a.size * a.dtype.itemsize for a in args) + sum(o.size * o.dtype.itemsize for o in outs)
        specs = [pl.BlockSpec(memory_space=pltpu.SMEM)] * scalars
        specs += [pl.BlockSpec(memory_space=pltpu.VMEM)] * (len(args) - scalars)
        return pl.pallas_call(
            body,
            out_shape=tuple(outs),
            in_specs=specs,
            out_specs=tuple(pl.BlockSpec(memory_space=pltpu.VMEM) for _ in outs),
            scratch_shapes=list(scratch),
            compiler_params=pltpu.CompilerParams(vmem_limit_bytes=16 * 1024 * 1024),
            cost_estimate=pl.CostEstimate(flops=flops, bytes_accessed=size, transcendentals=0),
        )(*args)

    return run


def f32(*shape):
    return jax.ShapeDtypeStruct(shape, jnp.float32)


def split(value):
    high = value.astype(jnp.bfloat16)
    return high, (value - high.astype(jnp.float32)).astype(jnp.bfloat16)


def dot(a, b, dims):
    return lax.dot_general(a, b, (dims, ((), ())), preferred_element_type=jnp.float32)


def records_body(own_ref, inv_ref, inno_ref, out_ref, pad_ref):
    count = own_ref.shape[1]
    tiles = out_ref.shape[0] // CAP
    chips = tiles // 2
    own = own_ref[...]
    owners = lax.broadcasted_iota(jnp.int32, (tiles, count), 0)
    onehot = jnp.where(owners == own, 1.0, 0.0)
    at = lax.broadcasted_iota(jnp.int32, (count, count), 0)
    to = lax.broadcasted_iota(jnp.int32, (count, count), 1)
    before = jnp.where(at < to, 1.0, 0.0).astype(jnp.bfloat16)
    earlier = dot(onehot.astype(jnp.bfloat16), before, ((1,), (0,)))
    rank = jnp.sum(onehot * earlier, axis=0, keepdims=True)
    chip_here = lax.broadcasted_iota(jnp.int32, (chips, count), 0) == (own >> 1)
    even = (own & 1) == 0
    picks = []
    for r in range(CAP):
        hit = jnp.where(chip_here & (rank == float(r)), 1.0, 0.0)
        picks.append(jnp.concatenate([jnp.where(even, hit, 0.0), jnp.where(even, 0.0, hit)], axis=1))
    pick = jnp.concatenate(picks, axis=0).astype(jnp.bfloat16)
    inv = inv_ref[...]
    pad_ref[...] = jnp.zeros_like(pad_ref)
    pad_ref[0:CHAN, :] = inv
    pad_ref[FULL : FULL + CHAN, :] = inv * inno_ref[...]
    zero = jnp.zeros((2 * WIN, count), jnp.float32)
    for core in range(2):
        at = LOW * core
        both = jnp.concatenate([pad_ref[at : at + WIN, :], pad_ref[FULL + at : FULL + at + WIN, :]], axis=0)
        block = jnp.concatenate(
            [jnp.concatenate([both, zero], axis=1), jnp.concatenate([zero, both], axis=1)], axis=0
        )
        first, rest = block.astype(jnp.bfloat16), block
        rest = rest - first.astype(jnp.float32)
        second, third = split(rest)
        total = dot(pick, first, ((1,), (1,)))
        total = total + dot(pick, second, ((1,), (1,)))
        total = total + dot(pick, third, ((1,), (1,)))
        for r in range(CAP):
            out_ref[pl.ds(core * CAP + r, chips, stride=2 * CAP), :] = total[r * chips : (r + 1) * chips]


def fields_body(core_ref, diff_ref, mask_ref, cell_ref, corner_ref, mine_ref, mate_ref, pad_ref):
    core = core_ref[0]
    slots = cell_ref.shape[1]
    masked = diff_ref[...] * mask_ref[...].astype(jnp.float32)[None]
    pad_ref[0 : CHAN * CY, :] = masked.reshape(CHAN * CY, COLS)
    pad_ref[CHAN * CY :, :] = jnp.zeros((FULL * CY - CHAN * CY, COLS), jnp.float32)
    for r in range(CY):
        at = LOW * CY * core + r
        mine_ref[r] = pad_ref[pl.ds(at, WIN, stride=CY), :]
        at = LOW * CY * (1 - core) + r
        mate_ref[r * WIN : (r + 1) * WIN, :] = pad_ref[pl.ds(at, WIN, stride=CY), :]
    base = CY * WIN
    table = jnp.concatenate(
        [cell_ref[...].astype(jnp.float32), corner_ref[...], jnp.zeros((3, slots), jnp.float32)], axis=0
    )
    for part in range(slots // COLS):
        mate_ref[base + 8 * part : base + 8 * part + 8, :] = table[:, part * COLS : (part + 1) * COLS]


def adjoint(misfits, high_ref, low_ref, store):
    for tile in range(2):
        high, low = split(misfits[tile])
        both = jnp.concatenate([high, low], axis=0)
        wide = dot(both, high_ref[tile], ((1,), (1,)))
        flat = wide[:WIN] + wide[WIN:] + dot(high, low_ref[tile], ((1,), (1,)))
        for r in range(CY):
            store(tile * CY + r, flat[:, r * COLS : (r + 1) * COLS])


def seed_body(core_ref, mine_ref, theirs_ref, cell_ref, corner_ref, rec_ref, *outs):
    d_ref, high_ref, low_ref, weight_ref, g_ref, up_ref, down_ref = outs
    core = core_ref[0]
    slots = cell_ref.shape[1]
    base = CY * WIN
    other = jnp.concatenate(
        [theirs_ref[base + 8 * part : base + 8 * part + 8, :] for part in range(slots // COLS)], axis=1
    )
    here = jnp.concatenate(
        [cell_ref[...].astype(jnp.float32), corner_ref[...], jnp.zeros((3, slots), jnp.float32)], axis=0
    )
    columns = lax.broadcasted_iota(jnp.int32, (COLS, slots), 0)
    slot_t = rec_ref[...].T
    targets = []
    for tile in range(2):
        first = core == tile
        table = jnp.where(first, here, other)
        cell = table[0:1].astype(jnp.int32)
        row = jnp.zeros_like(cell)
        for edge in range(1, CY - 1):
            row = row + jnp.where(cell >= edge * (COLS - 1), 1, 0)
        col = cell - row * (COLS - 1)
        at_col, at_next = col == columns, col + 1 == columns
        for r in range(CY):
            lower, upper = row == r, row == r - 1
            west = jnp.where(lower, table[1:2], 0.0) + jnp.where(upper, table[3:4], 0.0)
            east = jnp.where(lower, table[2:3], 0.0) + jnp.where(upper, table[4:5], 0.0)
            matrix = jnp.where(at_col, west, 0.0) + jnp.where(at_next, east, 0.0)
            high, low = split(matrix)
            high_ref[tile, r * COLS : (r + 1) * COLS, :] = high
            low_ref[tile, r * COLS : (r + 1) * COLS, :] = low
            d_ref[tile * CY + r] = jnp.where(first, mine_ref[r], theirs_ref[r * WIN : (r + 1) * WIN, :])
        weight_ref[tile] = slot_t[tile * 2 * WIN : tile * 2 * WIN + WIN]
        targets.append(slot_t[tile * 2 * WIN + WIN : (tile + 1) * 2 * WIN])

    def store(row, value):
        g_ref[row] = jnp.sqrt(d_ref[row]) * value

    adjoint(targets, high_ref, low_ref, store)
    up_ref[0:FAR] = g_ref[0:FAR]
    up_ref[FAR : 2 * FAR] = d_ref[0:FAR]
    down_ref[0:FAR] = g_ref[ROWS - FAR : ROWS]
    down_ref[FAR : 2 * FAR] = d_ref[ROWS - FAR : ROWS]


def places(halo):
    each = COLS // halo
    rows = range(1, ROWS + 2 * halo - 1)
    return [(row, n // each, n % each) for n, row in enumerate(rows)], -(-len(rows) // each)


def strips_body(halo, kinds, *refs):
    heres, (south_ref, north_ref, west_ref, east_ref) = refs[:kinds], refs[kinds:]
    spots, tiles = places(halo)
    lane = lax.broadcasted_iota(jnp.int32, (WIN, COLS), 1)
    for kind in range(kinds):
        for tile in range(tiles):
            west = jnp.zeros((WIN, COLS), jnp.float32)
            east = jnp.zeros((WIN, COLS), jnp.float32)
            for row, own_tile, q in spots:
                if own_tile != tile:
                    continue
                if row < halo:
                    line = south_ref[kind * halo + row]
                elif row < halo + ROWS:
                    line = heres[kind][row - halo]
                else:
                    line = north_ref[kind * halo + row - halo - ROWS]
                inside = (lane >= halo * q) & (lane < halo * q + halo)
                west = jnp.where(inside, pltpu.roll(line, halo * q, 1) if q else line, west)
                east = jnp.where(inside, pltpu.roll(line, (halo * q + halo) % COLS, 1), east)
            west_ref[kind * tiles + tile] = west
            east_ref[kind * tiles + tile] = east


def extend(dst, halo, offset, kind, here_ref, south_ref, north_ref, east_ref, west_ref):
    spots, tiles = places(halo)
    where_of = {row: (tile, q) for row, tile, q in spots}
    lane = lax.broadcasted_iota(jnp.int32, (WIN, COLS), 1)
    for row in range(ROWS + 2 * halo):
        if row < halo:
            line = south_ref[kind * halo + row]
        elif row < halo + ROWS:
            line = here_ref[row - halo]
        else:
            line = north_ref[kind * halo + row - halo - ROWS]
        dst[offset + row, :, 0:COLS] = line
        beyond = jnp.zeros((WIN, COLS), jnp.float32)
        if row in where_of:
            tile, q = where_of[row]
            right, left = east_ref[kind * tiles + tile], west_ref[kind * tiles + tile]
            right = pltpu.roll(right, COLS - halo * q, 1) if q else right
            left = pltpu.roll(left, COLS - halo - halo * q, 1)
            beyond = jnp.where(lane < halo, right, jnp.where(lane >= COLS - halo, left, 0.0))
        dst[offset + row, :, COLS:] = beyond


def sweep(src, dst, d_ref, low, high):
    lane = lax.broadcasted_iota(jnp.int32, (WIN, COLS), 1)
    last, first = lane == COLS - 1, lane == 0

    def body(row, carry):
        before, now = carry
        after = src[row + 1]
        a, b = now[:, :COLS], now[:, COLS:]
        east_a, east_b = pltpu.roll(a, COLS - 1, 1), pltpu.roll(b, COLS - 1, 1)
        west_a, west_b = pltpu.roll(a, 1, 1), pltpu.roll(b, 1, 1)
        beside_a = jnp.where(last, east_b, east_a) + jnp.where(first, west_b, west_a)
        beside_b = jnp.where(last, east_a, east_b) + jnp.where(first, west_a, west_b)
        beside = jnp.concatenate([beside_a, beside_b], axis=1)
        dst[row] = now + d_ref[row] * (before + after + beside - 4.0 * now)
        return now, after

    lax.fori_loop(low, high, body, (src[low - 1], src[low]), unroll=2)


def unscale(value, d):
    return jnp.where(d > 0.0, value * lax.rsqrt(jnp.where(d > 0.0, d, 1.0)), 0.0)


def largest(value):
    top = jnp.max(jnp.max(jnp.abs(value), axis=1, keepdims=True), axis=0, keepdims=True)
    return jnp.maximum(top, 1e-30)


def whole_sum(value):
    return jnp.sum(jnp.sum(value, axis=1, keepdims=True), axis=0, keepdims=True)


def pair_body(later, *refs):
    refs = list(refs)
    core_ref = refs.pop(0)
    here_ref, south_ref, north_ref, east_ref, west_ref = refs[:5]
    refs = refs[5:]
    if later:
        wide_d, high_ref, low_ref, weight_ref, q_in, u_in = refs[:6]
        q_ref, up_ref, down_ref, g_ref, stats_ref, first_ref, second_ref = refs[6:]
    else:
        d_ref, high_ref, low_ref, weight_ref = refs[:4]
        q_ref, u_ref, wide_d, up_ref, down_ref, g_ref, first_ref, second_ref = refs[4:]
        extend(wide_d, FAR, 0, 1, d_ref, south_ref, north_ref, east_ref, west_ref)
    extend(first_ref, FAR, 0, 0, here_ref, south_ref, north_ref, east_ref, west_ref)
    src, dst = first_ref, second_ref
    total = ROWS + 2 * FAR
    halo = STEPS if later else FAR
    rows = []
    for step in range(1, FAR + 1):
        sweep(src, dst, wide_d, step, total - step)
        src, dst = dst, src
        if step == STEPS:
            for r in range(ROWS):
                value = unscale(src[FAR + r, :, 0:COLS], wide_d[FAR + r, :, 0:COLS])
                q_ref[r] = q_in[r] + value if later else value
    for r in range(ROWS):
        value = unscale(src[FAR + r, :, 0:COLS], wide_d[FAR + r, :, 0:COLS])
        if later:
            value = value + u_in[r]
        else:
            u_ref[r] = value
        rows.append(value)
    misfits, samples = [], []
    for tile in range(2):
        flat = jnp.concatenate(rows[tile * CY : (tile + 1) * CY], axis=1)
        high, low = split(flat)
        both = dot(jnp.concatenate([high, low], axis=0), high_ref[tile], ((1,), (0,)))
        value = both[:WIN] + both[WIN:] + dot(high, low_ref[tile], ((1,), (0,)))
        samples.append(value)
        misfits.append(weight_ref[tile] * value)

    def store(row, value):
        g_ref[row] = jnp.sqrt(wide_d[FAR + row, :, 0:COLS]) * value

    adjoint(misfits, high_ref, low_ref, store)
    up_ref[...] = g_ref[0:halo]
    down_ref[...] = g_ref[ROWS - halo : ROWS]
    if later:
        sub = lax.broadcasted_iota(jnp.int32, (WIN, 1), 0)
        keep = jnp.where((sub < LOW) | (core_ref[0] == 1), 1.0, 0.0)
        top0 = jnp.zeros((WIN, COLS), jnp.float32)
        top1 = jnp.zeros((WIN, COLS), jnp.float32)
        for r in range(ROWS):
            top0 = jnp.maximum(top0, jnp.abs(q_in[r]))
            top1 = jnp.maximum(top1, jnp.abs(q_ref[r]))
        t0, t1 = largest(top0), largest(top1)
        v1 = jnp.maximum(largest(samples[0]), largest(samples[1]))
        i0, i1, iv = 1.0 / t0, 1.0 / t1, 1.0 / v1
        sums = [jnp.zeros((WIN, COLS), jnp.float32) for _ in range(3)]
        for r in range(ROWS):
            a, b = q_in[r] * i0, q_ref[r] * i1
            sums = [sums[0] + a * a, sums[1] + a * b, sums[2] + b * b]
        values = [whole_sum(s * keep) for s in sums]
        quad = sum(weight_ref[tile] * (samples[tile] * iv) * (samples[tile] * iv) for tile in range(2))
        values += [whole_sum(quad * keep), t0, t1, v1]
        stats_ref[...] = jnp.broadcast_to(as_row(values), stats_ref.shape)


def as_row(values):
    lane = lax.broadcasted_iota(jnp.int32, (1, COLS), 1)
    row = jnp.zeros((1, COLS), jnp.float32)
    for n, value in enumerate(values):
        row = jnp.where(lane == n, value, row)
    return row


def merged(block):
    part = [block[:, n : n + 1] for n in range(7)]
    tops = [jnp.max(part[n], axis=0, keepdims=True) for n in (4, 5, 6)]
    r0, r1, rv = (part[4 + n] / tops[n] for n in range(3))
    values = [part[0] * r0 * r0, part[1] * r0 * r1, part[2] * r1 * r1, part[3] * rv * rv]
    return [jnp.sum(value, axis=0, keepdims=True) for value in values] + tops


def merge_body(in_ref, out_ref):
    out_ref[...] = jnp.broadcast_to(as_row(merged(in_ref[...])), out_ref.shape)


def last_body(core_ref, here_ref, south_ref, north_ref, east_ref, west_ref, wide_d, q0_ref, q1_ref, *outs):
    mine_ref, mate_ref, first_ref, second_ref, near_d, q2_ref = outs
    core = core_ref[0]
    total = ROWS + 2 * STEPS
    extend(first_ref, STEPS, 0, 0, here_ref, south_ref, north_ref, east_ref, west_ref)
    for row in range(total):
        near_d[row] = wide_d[row + FAR - STEPS]
    src, dst = first_ref, second_ref
    for step in range(1, STEPS + 1):
        sweep(src, dst, near_d, step, total - step)
        src, dst = dst, src
    for r in range(ROWS):
        d = near_d[STEPS + r, :, 0:COLS]
        q2_ref[r] = q1_ref[r] + unscale(src[STEPS + r, :, 0:COLS], d)
    for n, q in enumerate((q0_ref, q1_ref, q2_ref)):
        mine_ref[n * CY : (n + 1) * CY] = q[pl.ds(core * CY, CY)]
        mate_ref[n * CY : (n + 1) * CY] = q[pl.ds((1 - core) * CY, CY)]


def final_body(core_ref, mine_ref, theirs_ref, stats_ref, control_ref, residual_ref, c_ref, r_ref):
    core = core_ref[0]
    m00, m01, m11, s11, t0, t1, v1 = merged(stats_ref[...])
    ratio = t1 / t0
    scaled = m00 / m01
    alpha0 = scaled / ratio
    norm1 = m00 - 2.0 * scaled * m01 + scaled * scaled * m11
    beta = norm1 / m00
    lift = 1.0 + beta
    relative = v1 / t1
    curve = lift * lift * ratio * m01 - 2.0 * lift * scaled * ratio * m11
    curve = curve + scaled * scaled * (m11 + relative * relative * s11)
    alpha1 = norm1 / curve
    one = alpha0 + alpha1 * lift
    two = alpha1 * alpha0
    for ref, owner in ((mine_ref, core), (theirs_ref, 1 - core)):
        for r in range(CY):
            q0, q1, q2 = ref[r], ref[CY + r], ref[2 * CY + r]
            at = LOW * CY * owner + r
            c_ref[pl.ds(at, WIN, stride=CY), :] = one * q0 - two * q1
            r_ref[pl.ds(at, WIN, stride=CY), :] = q0 - one * q1 + two * q2
    control_ref[...] = c_ref[0 : CHAN * CY, :].reshape(CHAN, CY, COLS)
    residual_ref[...] = r_ref[0 : CHAN * CY, :].reshape(CHAN, CY, COLS)


def on_device(
    diffusivity, land_mask, innovation, inverse_variance, owner_ids, cell_index, corner_weights
):
    count_x, count_y = lax.axis_size("gx"), lax.axis_size("gy")
    slots = count_y * CAP
    core = (lax.axis_index("gy") % 2).astype(jnp.int32).reshape(1)
    corners = corner_weights.reshape(4, slots)
    count = owner_ids.shape[0]

    def along_y(value, by):
        pairs = [(i, i + by) for i in range(count_y) if 0 <= i + by < count_y]
        return lax.ppermute(value, "gy", pairs)

    def along_x(value, by):
        return lax.ppermute(value, "gx", [(i, (i + by) % count_x) for i in range(count_x)])

    def across(value):
        return lax.ppermute(value, "gy", [(i, i ^ 1) for i in range(count_y)])

    def exchange(heres, up, down, halo):
        kinds = len(heres)
        tiles = places(halo)[1]
        south, north = along_y(down, 2), along_y(up, -2)
        pack = call(functools.partial(strips_body, halo, kinds), [f32(kinds * tiles, WIN, COLS)] * 2, 10**6)
        west, east = pack(*heres, south, north)
        return south, north, along_x(west, -1), along_x(east, 1)

    field = f32(ROWS, WIN, COLS)
    (chunks,) = call(
        records_body, [f32(slots, COLS)], 10**7, [pltpu.VMEM((2 * FULL, count), jnp.float32)]
    )(owner_ids.reshape(1, count), inverse_variance, innovation)
    mine, mate = call(
        fields_body,
        [f32(CY, WIN, COLS), f32(CY * WIN + 8 * (slots // COLS), COLS)],
        10**6,
        [pltpu.VMEM((FULL * CY, COLS), jnp.float32)],
        1,
    )(core, diffusivity, land_mask, cell_index, corners)
    theirs = across(mate)
    received = lax.all_to_all(chunks, "gy", split_axis=0, concat_axis=0, tiled=True)
    matrix = jax.ShapeDtypeStruct((2, CY * COLS, slots), jnp.bfloat16)
    both = f32(2 * FAR, WIN, COLS)
    d, high, low, weights, g, up, down = call(
        seed_body, [field, matrix, matrix, f32(2, WIN, slots), field, both, both], 10**8, (), 1
    )(core, mine, theirs, cell_index, corners, received)
    wide = (ROWS + 2 * FAR, WIN, 2 * COLS)
    space = [pltpu.VMEM(wide, jnp.float32)] * 2
    south, north, east, west = exchange([g, d], up, down, FAR)
    q0, u0, wide_d, up, down, g = call(
        functools.partial(pair_body, False),
        [field, field, f32(*wide), f32(FAR, WIN, COLS), f32(FAR, WIN, COLS), field],
        2 * 10**8,
        space,
        1,
    )(core, g, south, north, east, west, d, high, low, weights)
    south, north, east, west = exchange([g], up, down, FAR)
    q1, up, down, g, stats = call(
        functools.partial(pair_body, True),
        [field, f32(STEPS, WIN, COLS), f32(STEPS, WIN, COLS), field, f32(count_y, COLS)],
        2 * 10**8,
        space,
        1,
    )(core, g, south, north, east, west, wide_d, high, low, weights, q0, u0)
    stats = lax.all_to_all(stats, "gy", split_axis=0, concat_axis=0, tiled=True)
    (stats,) = call(merge_body, [f32(count_x, COLS)], 10**5)(stats)
    stats = lax.all_to_all(stats, "gx", split_axis=0, concat_axis=0, tiled=True)
    south, north, east, west = exchange([g], up, down, STEPS)
    near = (ROWS + 2 * STEPS, WIN, 2 * COLS)
    mine, mate = call(
        last_body,
        [f32(3 * CY, WIN, COLS)] * 2,
        10**8,
        [pltpu.VMEM(near, jnp.float32)] * 3 + [pltpu.VMEM((ROWS, WIN, COLS), jnp.float32)],
        1,
    )(core, g, south, north, east, west, wide_d, q0, q1)
    theirs = across(mate)
    out = f32(CHAN, CY, COLS)
    return call(
        final_body, [out, out], 10**6, [pltpu.VMEM((FULL * CY, COLS), jnp.float32)] * 2, 1
    )(core, mine, theirs, stats)


def solution(mesh):
    return jax.shard_map(
        on_device,
        mesh=mesh,
        in_specs=(
            P(None, "gy", "gx"),
            P("gy", "gx"),
            P(None, ("gx", "gy")),
            P(None, ("gx", "gy")),
            P(("gx", "gy"), None),
            P(("gx", "gy"), None),
            P(None, ("gx", "gy"), None),
        ),
        out_specs=(P(None, "gy", "gx"), P(None, "gy", "gx")),
        check_vma=False,
    )
```

```python
import functools

import jax
import jax.numpy as jnp
from jax import lax
from jax.experimental import pallas as pl
from jax.experimental.pallas import tpu as pltpu
from jax.sharding import PartitionSpec as P

CAP = 4
STEPS = 5
CHAN = 50
WIN = 32
LOW = 24
FULL = 56
COLS = 128
CY = 8
ROWS = 2 * CY
FAR = 2 * STEPS


def call(body, outs, flops, scratch=(), scalars=0, source=pltpu.VMEM):
    def run(*args):
        size = sum(a.size * a.dtype.itemsize for a in args) + sum(o.size * o.dtype.itemsize for o in outs)
        specs = [pl.BlockSpec(memory_space=pltpu.SMEM)] * scalars
        specs += [pl.BlockSpec(memory_space=source)] * (len(args) - scalars)
        return pl.pallas_call(
            body,
            out_shape=tuple(outs),
            in_specs=specs,
            out_specs=tuple(pl.BlockSpec(memory_space=pltpu.VMEM) for _ in outs),
            scratch_shapes=list(scratch),
            compiler_params=pltpu.CompilerParams(vmem_limit_bytes=16 * 1024 * 1024),
            cost_estimate=pl.CostEstimate(flops=flops, bytes_accessed=size, transcendentals=0),
        )(*args)

    return run


def f32(*shape):
    return jax.ShapeDtypeStruct(shape, jnp.float32)


def split(value):
    high = value.astype(jnp.bfloat16)
    return high, (value - high.astype(jnp.float32)).astype(jnp.bfloat16)


def dot(a, b, dims):
    return lax.dot_general(a, b, (dims, ((), ())), preferred_element_type=jnp.float32)


def first_body(core_ref, *refs):
    ins, (chunk_ref, mine_ref, mate_ref, table_ref), space = refs[:7], refs[7:11], refs[11:]
    held, pad_ref, field_ref, sems = space[:7], space[7], space[8], space[9]
    copies = [pltpu.make_async_copy(ins[n], held[n], sems.at[n]) for n in range(7)]
    for copy in copies:
        copy.start()
    own_ref, inv_ref, inno_ref, diff_ref, mask_ref, cell_ref, corner_ref = held
    for copy in copies:
        copy.wait()
    route(own_ref, inv_ref, inno_ref, chunk_ref, pad_ref)
    core = core_ref[0]
    slots = cell_ref.shape[1]
    masked = diff_ref[...] * mask_ref[...].astype(jnp.float32)[None]
    field_ref[0 : CHAN * CY, :] = masked.reshape(CHAN * CY, COLS)
    field_ref[CHAN * CY :, :] = jnp.zeros((FULL * CY - CHAN * CY, COLS), jnp.float32)
    for r in range(CY):
        at = LOW * CY * core + r
        mine_ref[r] = field_ref[pl.ds(at, WIN, stride=CY), :]
        at = LOW * CY * (1 - core) + r
        mate_ref[r * WIN : (r + 1) * WIN, :] = field_ref[pl.ds(at, WIN, stride=CY), :]
    base = CY * WIN
    rows = [cell_ref[...].astype(jnp.float32)] + [corner_ref[n] for n in range(4)]
    table = jnp.concatenate(rows + [jnp.zeros((3, slots), jnp.float32)], axis=0)
    table_ref[...] = table
    for part in range(slots // COLS):
        mate_ref[base + 8 * part : base + 8 * part + 8, :] = table[:, part * COLS : (part + 1) * COLS]


def route(own_ref, inv_ref, inno_ref, out_ref, pad_ref):
    count = own_ref.shape[1]
    tiles = out_ref.shape[0] // CAP
    chips = tiles // 2
    own = own_ref[...]
    owners = lax.broadcasted_iota(jnp.int32, (tiles, count), 0)
    onehot = jnp.where(owners == own, 1.0, 0.0)
    at = lax.broadcasted_iota(jnp.int32, (count, count), 0)
    to = lax.broadcasted_iota(jnp.int32, (count, count), 1)
    before = jnp.where(at < to, 1.0, 0.0).astype(jnp.bfloat16)
    earlier = dot(onehot.astype(jnp.bfloat16), before, ((1,), (0,)))
    rank = jnp.sum(onehot * earlier, axis=0, keepdims=True)
    chip_here = lax.broadcasted_iota(jnp.int32, (chips, count), 0) == (own >> 1)
    even = (own & 1) == 0
    picks = []
    for r in range(CAP):
        hit = jnp.where(chip_here & (rank == float(r)), 1.0, 0.0)
        picks.append(jnp.concatenate([jnp.where(even, hit, 0.0), jnp.where(even, 0.0, hit)], axis=1))
    pick = jnp.concatenate(picks, axis=0).astype(jnp.bfloat16)
    inv = inv_ref[...]
    pad_ref[...] = jnp.zeros_like(pad_ref)
    pad_ref[0:CHAN, :] = inv
    pad_ref[FULL : FULL + CHAN, :] = inv * inno_ref[...]
    zero = jnp.zeros((2 * WIN, count), jnp.float32)
    for core in range(2):
        at = LOW * core
        both = jnp.concatenate([pad_ref[at : at + WIN, :], pad_ref[FULL + at : FULL + at + WIN, :]], axis=0)
        block = jnp.concatenate(
            [jnp.concatenate([both, zero], axis=1), jnp.concatenate([zero, both], axis=1)], axis=0
        )
        first, rest = block.astype(jnp.bfloat16), block
        rest = rest - first.astype(jnp.float32)
        second, third = split(rest)
        total = dot(pick, first, ((1,), (1,)))
        total = total + dot(pick, second, ((1,), (1,)))
        total = total + dot(pick, third, ((1,), (1,)))
        for r in range(CAP):
            out_ref[pl.ds(core * CAP + r, chips, stride=2 * CAP), :] = total[r * chips : (r + 1) * chips]


def adjoint(misfits, high_ref, low_ref, store):
    for tile in range(2):
        high, low = split(misfits[tile])
        both = jnp.concatenate([high, low], axis=0)
        wide = dot(both, high_ref[tile], ((1,), (1,)))
        flat = wide[:WIN] + wide[WIN:] + dot(high, low_ref[tile], ((1,), (1,)))
        for r in range(CY):
            store(tile * CY + r, flat[:, r * COLS : (r + 1) * COLS])


def seed_body(core_ref, mine_ref, theirs_ref, table_ref, rec_ref, *outs):
    d_ref, high_ref, low_ref, weight_ref, g_ref, up_ref, down_ref = outs
    core = core_ref[0]
    slots = table_ref.shape[1]
    base = CY * WIN
    other = jnp.concatenate(
        [theirs_ref[base + 8 * part : base + 8 * part + 8, :] for part in range(slots // COLS)], axis=1
    )
    here = table_ref[...]
    columns = lax.broadcasted_iota(jnp.int32, (COLS, slots), 0)
    slot_t = rec_ref[...].T
    targets = []
    for tile in range(2):
        first = core == tile
        table = jnp.where(first, here, other)
        cell = table[0:1].astype(jnp.int32)
        row = jnp.zeros_like(cell)
        for edge in range(1, CY - 1):
            row = row + jnp.where(cell >= edge * (COLS - 1), 1, 0)
        col = cell - row * (COLS - 1)
        at_col, at_next = col == columns, col + 1 == columns
        for r in range(CY):
            lower, upper = row == r, row == r - 1
            west = jnp.where(lower, table[1:2], 0.0) + jnp.where(upper, table[3:4], 0.0)
            east = jnp.where(lower, table[2:3], 0.0) + jnp.where(upper, table[4:5], 0.0)
            matrix = jnp.where(at_col, west, 0.0) + jnp.where(at_next, east, 0.0)
            high, low = split(matrix)
            high_ref[tile, r * COLS : (r + 1) * COLS, :] = high
            low_ref[tile, r * COLS : (r + 1) * COLS, :] = low
            d_ref[tile * CY + r] = jnp.where(first, mine_ref[r], theirs_ref[r * WIN : (r + 1) * WIN, :])
        weight_ref[tile] = slot_t[tile * 2 * WIN : tile * 2 * WIN + WIN]
        targets.append(slot_t[tile * 2 * WIN + WIN : (tile + 1) * 2 * WIN])

    def store(row, value):
        g_ref[row] = jnp.sqrt(d_ref[row]) * value

    adjoint(targets, high_ref, low_ref, store)
    up_ref[0:FAR] = g_ref[0:FAR]
    up_ref[FAR : 2 * FAR] = d_ref[0:FAR]
    down_ref[0:FAR] = g_ref[ROWS - FAR : ROWS]
    down_ref[FAR : 2 * FAR] = d_ref[ROWS - FAR : ROWS]


def places(halo):
    each = COLS // halo
    rows = range(1, ROWS + 2 * halo - 1)
    return [(row, n // each, n % each) for n, row in enumerate(rows)], -(-len(rows) // each)


def strips_body(halo, kinds, *refs):
    heres, (south_ref, north_ref, west_ref, east_ref) = refs[:kinds], refs[kinds:]
    spots, tiles = places(halo)
    lane = lax.broadcasted_iota(jnp.int32, (WIN, COLS), 1)
    for kind in range(kinds):
        for tile in range(tiles):
            west = jnp.zeros((WIN, COLS), jnp.float32)
            east = jnp.zeros((WIN, COLS), jnp.float32)
            for row, own_tile, q in spots:
                if own_tile != tile:
                    continue
                if row < halo:
                    line = south_ref[kind * halo + row]
                elif row < halo + ROWS:
                    line = heres[kind][row - halo]
                else:
                    line = north_ref[kind * halo + row - halo - ROWS]
                inside = (lane >= halo * q) & (lane < halo * q + halo)
                west = jnp.where(inside, pltpu.roll(line, halo * q, 1) if q else line, west)
                east = jnp.where(inside, pltpu.roll(line, (halo * q + halo) % COLS, 1), east)
            west_ref[kind * tiles + tile] = west
            east_ref[kind * tiles + tile] = east


def extend(dst, halo, offset, kind, here_ref, south_ref, north_ref, east_ref, west_ref):
    spots, tiles = places(halo)
    where_of = {row: (tile, q) for row, tile, q in spots}
    lane = lax.broadcasted_iota(jnp.int32, (WIN, COLS), 1)
    for row in range(ROWS + 2 * halo):
        if row < halo:
            line = south_ref[kind * halo + row]
        elif row < halo + ROWS:
            line = here_ref[row - halo]
        else:
            line = north_ref[kind * halo + row - halo - ROWS]
        dst[offset + row, :, 0:COLS] = line
        beyond = jnp.zeros((WIN, COLS), jnp.float32)
        if row in where_of:
            tile, q = where_of[row]
            right, left = east_ref[kind * tiles + tile], west_ref[kind * tiles + tile]
            right = pltpu.roll(right, COLS - halo * q, 1) if q else right
            left = pltpu.roll(left, COLS - halo - halo * q, 1)
            beyond = jnp.where(lane < halo, right, jnp.where(lane >= COLS - halo, left, 0.0))
        dst[offset + row, :, COLS:] = beyond


def sweep(src, dst, d_ref, low, high):
    lane = lax.broadcasted_iota(jnp.int32, (WIN, COLS), 1)
    last, first = lane == COLS - 1, lane == 0

    def body(row, carry):
        before, now = carry
        after = src[row + 1]
        a, b = now[:, :COLS], now[:, COLS:]
        east_a, east_b = pltpu.roll(a, COLS - 1, 1), pltpu.roll(b, COLS - 1, 1)
        west_a, west_b = pltpu.roll(a, 1, 1), pltpu.roll(b, 1, 1)
        beside_a = jnp.where(last, east_b, east_a) + jnp.where(first, west_b, west_a)
        beside_b = jnp.where(last, east_a, east_b) + jnp.where(first, west_a, west_b)
        beside = jnp.concatenate([beside_a, beside_b], axis=1)
        dst[row] = now + d_ref[row] * (before + after + beside - 4.0 * now)
        return now, after

    carry = (src[low - 1], src[low])
    for row in range(low, high):
        carry = body(row, carry)


def unscale(value, d):
    return jnp.where(d > 0.0, value * lax.rsqrt(jnp.where(d > 0.0, d, 1.0)), 0.0)


def largest(value):
    top = jnp.max(jnp.max(jnp.abs(value), axis=1, keepdims=True), axis=0, keepdims=True)
    return jnp.maximum(top, 1e-30)


def whole_sum(value):
    return jnp.sum(jnp.sum(value, axis=1, keepdims=True), axis=0, keepdims=True)


def pair_body(later, *refs):
    refs = list(refs)
    core_ref = refs.pop(0)
    here_ref, south_ref, north_ref, east_ref, west_ref = refs[:5]
    refs = refs[5:]
    if later:
        wide_d, high_ref, low_ref, weight_ref, q_in, u_in = refs[:6]
        q_ref, up_ref, down_ref, g_ref, stats_ref, first_ref, second_ref = refs[6:]
    else:
        d_ref, high_ref, low_ref, weight_ref = refs[:4]
        q_ref, u_ref, wide_d, up_ref, down_ref, g_ref, first_ref, second_ref = refs[4:]
        extend(wide_d, FAR, 0, 1, d_ref, south_ref, north_ref, east_ref, west_ref)
    extend(first_ref, FAR, 0, 0, here_ref, south_ref, north_ref, east_ref, west_ref)
    src, dst = first_ref, second_ref
    total = ROWS + 2 * FAR
    halo = STEPS if later else FAR
    rows = []
    for step in range(1, FAR + 1):
        sweep(src, dst, wide_d, step, total - step)
        src, dst = dst, src
        if step == STEPS:
            for r in range(ROWS):
                value = unscale(src[FAR + r, :, 0:COLS], wide_d[FAR + r, :, 0:COLS])
                q_ref[r] = q_in[r] + value if later else value
    for r in range(ROWS):
        value = unscale(src[FAR + r, :, 0:COLS], wide_d[FAR + r, :, 0:COLS])
        if later:
            value = value + u_in[r]
        else:
            u_ref[r] = value
        rows.append(value)
    misfits, samples = [], []
    for tile in range(2):
        flat = jnp.concatenate(rows[tile * CY : (tile + 1) * CY], axis=1)
        high, low = split(flat)
        both = dot(jnp.concatenate([high, low], axis=0), high_ref[tile], ((1,), (0,)))
        value = both[:WIN] + both[WIN:] + dot(high, low_ref[tile], ((1,), (0,)))
        samples.append(value)
        misfits.append(weight_ref[tile] * value)

    def store(row, value):
        g_ref[row] = jnp.sqrt(wide_d[FAR + row, :, 0:COLS]) * value

    adjoint(misfits, high_ref, low_ref, store)
    up_ref[...] = g_ref[0:halo]
    down_ref[...] = g_ref[ROWS - halo : ROWS]
    if later:
        sub = lax.broadcasted_iota(jnp.int32, (WIN, 1), 0)
        keep = jnp.where((sub < LOW) | (core_ref[0] == 1), 1.0, 0.0)
        top0 = jnp.zeros((WIN, COLS), jnp.float32)
        top1 = jnp.zeros((WIN, COLS), jnp.float32)
        for r in range(ROWS):
            top0 = jnp.maximum(top0, jnp.abs(q_in[r]))
            top1 = jnp.maximum(top1, jnp.abs(q_ref[r]))
        t0, t1 = largest(top0), largest(top1)
        v1 = jnp.maximum(largest(samples[0]), largest(samples[1]))
        i0, i1, iv = 1.0 / t0, 1.0 / t1, 1.0 / v1
        sums = [jnp.zeros((WIN, COLS), jnp.float32) for _ in range(3)]
        for r in range(ROWS):
            a, b = q_in[r] * i0, q_ref[r] * i1
            sums = [sums[0] + a * a, sums[1] + a * b, sums[2] + b * b]
        values = [whole_sum(s * keep) for s in sums]
        quad = sum(weight_ref[tile] * (samples[tile] * iv) * (samples[tile] * iv) for tile in range(2))
        values += [whole_sum(quad * keep), t0, t1, v1]
        stats_ref[...] = jnp.broadcast_to(as_row(values), stats_ref.shape)


def as_row(values):
    lane = lax.broadcasted_iota(jnp.int32, (1, COLS), 1)
    row = jnp.zeros((1, COLS), jnp.float32)
    for n, value in enumerate(values):
        row = jnp.where(lane == n, value, row)
    return row


def merged(block):
    part = [block[:, n : n + 1] for n in range(7)]
    tops = [jnp.max(part[n], axis=0, keepdims=True) for n in (4, 5, 6)]
    r0, r1, rv = (part[4 + n] / tops[n] for n in range(3))
    values = [part[0] * r0 * r0, part[1] * r0 * r1, part[2] * r1 * r1, part[3] * rv * rv]
    return [jnp.sum(value, axis=0, keepdims=True) for value in values] + tops


def merge_body(in_ref, out_ref):
    out_ref[...] = jnp.broadcast_to(as_row(merged(in_ref[...])), out_ref.shape)


def last_body(core_ref, here_ref, south_ref, north_ref, east_ref, west_ref, wide_d, q0_ref, q1_ref, *outs):
    mine_ref, mate_ref, first_ref, second_ref, near_d, q2_ref = outs
    core = core_ref[0]
    total = ROWS + 2 * STEPS
    extend(first_ref, STEPS, 0, 0, here_ref, south_ref, north_ref, east_ref, west_ref)
    for row in range(total):
        near_d[row] = wide_d[row + FAR - STEPS]
    src, dst = first_ref, second_ref
    for step in range(1, STEPS + 1):
        sweep(src, dst, near_d, step, total - step)
        src, dst = dst, src
    for r in range(ROWS):
        d = near_d[STEPS + r, :, 0:COLS]
        q2_ref[r] = q1_ref[r] + unscale(src[STEPS + r, :, 0:COLS], d)
    for n, q in enumerate((q0_ref, q1_ref, q2_ref)):
        mine_ref[n * CY : (n + 1) * CY] = q[pl.ds(core * CY, CY)]
        mate_ref[n * CY : (n + 1) * CY] = q[pl.ds((1 - core) * CY, CY)]


def final_body(core_ref, mine_ref, theirs_ref, stats_ref, control_ref, residual_ref, c_ref, r_ref):
    core = core_ref[0]
    m00, m01, m11, s11, t0, t1, v1 = merged(stats_ref[...])
    ratio = t1 / t0
    scaled = m00 / m01
    alpha0 = scaled / ratio
    norm1 = m00 - 2.0 * scaled * m01 + scaled * scaled * m11
    beta = norm1 / m00
    lift = 1.0 + beta
    relative = v1 / t1
    curve = lift * lift * ratio * m01 - 2.0 * lift * scaled * ratio * m11
    curve = curve + scaled * scaled * (m11 + relative * relative * s11)
    alpha1 = norm1 / curve
    one = alpha0 + alpha1 * lift
    two = alpha1 * alpha0
    for ref, owner in ((mine_ref, core), (theirs_ref, 1 - core)):
        for r in range(CY):
            q0, q1, q2 = ref[r], ref[CY + r], ref[2 * CY + r]
            at = LOW * CY * owner + r
            c_ref[pl.ds(at, WIN, stride=CY), :] = one * q0 - two * q1
            r_ref[pl.ds(at, WIN, stride=CY), :] = q0 - one * q1 + two * q2
    control_ref[...] = c_ref[0 : CHAN * CY, :].reshape(CHAN, CY, COLS)
    residual_ref[...] = r_ref[0 : CHAN * CY, :].reshape(CHAN, CY, COLS)


def on_device(
    diffusivity, land_mask, innovation, inverse_variance, owner_ids, cell_index, corner_weights
):
    count_x, count_y = lax.axis_size("gx"), lax.axis_size("gy")
    slots = count_y * CAP
    core = (lax.axis_index("gy") % 2).astype(jnp.int32).reshape(1)
    count = owner_ids.shape[0]

    def along_y(value, by):
        pairs = [(i, i + by) for i in range(count_y) if 0 <= i + by < count_y]
        return lax.ppermute(value, "gy", pairs)

    def along_x(value, by):
        return lax.ppermute(value, "gx", [(i, (i + by) % count_x) for i in range(count_x)])

    def across(value):
        return lax.ppermute(value, "gy", [(i, i ^ 1) for i in range(count_y)])

    def exchange(heres, up, down, halo, *after):
        kinds = len(heres)
        tiles = places(halo)[1]
        south, north = along_y(down, 2), along_y(up, -2)
        pack = call(functools.partial(strips_body, halo, kinds), [f32(kinds * tiles, WIN, COLS)] * 2, 10**6)
        west, east = pack(*heres, south, north)
        west, east, *after = lax.optimization_barrier((west, east, *after))
        return south, north, along_x(west, -1), along_x(east, 1), *after

    field = f32(ROWS, WIN, COLS)
    ins = [
        owner_ids.reshape(1, count), inverse_variance, innovation, diffusivity, land_mask, cell_index, corner_weights
    ]
    space = [pltpu.VMEM(x.shape, x.dtype) for x in ins]
    space += [pltpu.VMEM((2 * FULL, count), jnp.float32), pltpu.VMEM((FULL * CY, COLS), jnp.float32)]
    chunks, mine, mate, table = call(
        first_body,
        [f32(slots, COLS), f32(CY, WIN, COLS), f32(CY * WIN + 8 * (slots // COLS), COLS), f32(8, slots)],
        10**7,
        space + [pltpu.SemaphoreType.DMA((len(ins),))],
        1,
        pltpu.HBM,
    )(core, *(pltpu.with_memory_space_constraint(x, pltpu.HBM) for x in ins))
    theirs = across(mate)
    received = lax.all_to_all(chunks, "gy", split_axis=0, concat_axis=0, tiled=True)
    matrix = jax.ShapeDtypeStruct((2, CY * COLS, slots), jnp.bfloat16)
    both = f32(2 * FAR, WIN, COLS)
    d, high, low, weights, g, up, down = call(
        seed_body, [field, matrix, matrix, f32(2, WIN, slots), field, both, both], 10**8, (), 1
    )(core, mine, theirs, table, received)
    wide = (ROWS + 2 * FAR, WIN, 2 * COLS)
    space = [pltpu.VMEM(wide, jnp.float32)] * 2
    south, north, east, west = exchange([g, d], up, down, FAR)
    q0, u0, wide_d, up, down, g = call(
        functools.partial(pair_body, False),
        [field, field, f32(*wide), f32(FAR, WIN, COLS), f32(FAR, WIN, COLS), field],
        2 * 10**8,
        space,
        1,
    )(core, g, south, north, east, west, d, high, low, weights)
    south, north, east, west = exchange([g], up, down, FAR)
    q1, up, down, g, stats = call(
        functools.partial(pair_body, True),
        [field, f32(STEPS, WIN, COLS), f32(STEPS, WIN, COLS), field, f32(count_y, COLS)],
        2 * 10**8,
        space,
        1,
    )(core, g, south, north, east, west, wide_d, high, low, weights, q0, u0)
    stats = lax.all_to_all(stats, "gy", split_axis=0, concat_axis=0, tiled=True)
    (stats,) = call(merge_body, [f32(count_x, COLS)], 10**5)(stats)
    south, north, east, west, stats = exchange([g], up, down, STEPS, stats)
    stats = lax.all_to_all(stats, "gx", split_axis=0, concat_axis=0, tiled=True)
    near = (ROWS + 2 * STEPS, WIN, 2 * COLS)
    mine, mate = call(
        last_body,
        [f32(3 * CY, WIN, COLS)] * 2,
        10**8,
        [pltpu.VMEM(near, jnp.float32)] * 3 + [pltpu.VMEM((ROWS, WIN, COLS), jnp.float32)],
        1,
    )(core, g, south, north, east, west, wide_d, q0, q1)
    mate, stats = lax.optimization_barrier((mate, stats))
    theirs = across(mate)
    out = f32(CHAN, CY, COLS)
    return call(
        final_body, [out, out], 10**6, [pltpu.VMEM((FULL * CY, COLS), jnp.float32)] * 2, 1
    )(core, mine, theirs, stats)


def solution(mesh):
    return jax.shard_map(
        on_device,
        mesh=mesh,
        in_specs=(
            P(None, "gy", "gx"),
            P("gy", "gx"),
            P(None, ("gx", "gy")),
            P(None, ("gx", "gy")),
            P(("gx", "gy"), None),
            P(("gx", "gy"), None),
            P(None, ("gx", "gy"), None),
        ),
        out_specs=(P(None, "gy", "gx"), P(None, "gy", "gx")),
        check_vma=False,
    )
```

```python
import functools

import jax
import jax.numpy as jnp
from jax import lax
from jax.experimental import pallas as pl
from jax.experimental.pallas import tpu as pltpu
from jax.sharding import PartitionSpec as P

CAP = 4
STEPS = 5
CHAN = 50
WIN = 32
LOW = 24
FULL = 56
COLS = 128
CY = 8
ROWS = 2 * CY
FAR = 2 * STEPS


def call(body, outs, flops, scratch=(), scalars=0, source=pltpu.VMEM):
    def run(*args):
        size = sum(a.size * a.dtype.itemsize for a in args) + sum(o.size * o.dtype.itemsize for o in outs)
        specs = [pl.BlockSpec(memory_space=pltpu.SMEM)] * scalars
        specs += [pl.BlockSpec(memory_space=source)] * (len(args) - scalars)
        return pl.pallas_call(
            body,
            out_shape=tuple(outs),
            in_specs=specs,
            out_specs=tuple(pl.BlockSpec(memory_space=pltpu.VMEM) for _ in outs),
            scratch_shapes=list(scratch),
            compiler_params=pltpu.CompilerParams(vmem_limit_bytes=16 * 1024 * 1024),
            cost_estimate=pl.CostEstimate(flops=flops, bytes_accessed=size, transcendentals=0),
        )(*args)

    return run


def f32(*shape):
    return jax.ShapeDtypeStruct(shape, jnp.float32)


def split(value):
    high = value.astype(jnp.bfloat16)
    return high, (value - high.astype(jnp.float32)).astype(jnp.bfloat16)


def dot(a, b, dims):
    return lax.dot_general(a, b, (dims, ((), ())), preferred_element_type=jnp.float32)


def first_body(core_ref, *refs):
    ins, (chunk_ref, mine_ref, mate_ref, table_ref), space = refs[:7], refs[7:11], refs[11:]
    held, pad_ref, field_ref, sems = space[:7], space[7], space[8], space[9]
    copies = [pltpu.make_async_copy(ins[n], held[n], sems.at[n]) for n in range(7)]
    for copy in copies:
        copy.start()
    own_ref, inv_ref, inno_ref, diff_ref, mask_ref, cell_ref, corner_ref = held
    for copy in copies:
        copy.wait()
    route(own_ref, inv_ref, inno_ref, chunk_ref, pad_ref)
    core = core_ref[0]
    slots = cell_ref.shape[1]
    masked = diff_ref[...] * mask_ref[...].astype(jnp.float32)[None]
    field_ref[0 : CHAN * CY, :] = masked.reshape(CHAN * CY, COLS)
    field_ref[CHAN * CY :, :] = jnp.zeros((FULL * CY - CHAN * CY, COLS), jnp.float32)
    for r in range(CY):
        at = LOW * CY * core + r
        mine_ref[r] = field_ref[pl.ds(at, WIN, stride=CY), :]
        at = LOW * CY * (1 - core) + r
        mate_ref[r * WIN : (r + 1) * WIN, :] = field_ref[pl.ds(at, WIN, stride=CY), :]
    base = CY * WIN
    rows = [cell_ref[...].astype(jnp.float32)] + [corner_ref[n] for n in range(4)]
    table = jnp.concatenate(rows + [jnp.zeros((3, slots), jnp.float32)], axis=0)
    table_ref[...] = table
    for part in range(slots // COLS):
        mate_ref[base + 8 * part : base + 8 * part + 8, :] = table[:, part * COLS : (part + 1) * COLS]


def route(own_ref, inv_ref, inno_ref, out_ref, pad_ref):
    count = own_ref.shape[1]
    tiles = out_ref.shape[0] // CAP
    chips = tiles // 2
    own = own_ref[...]
    owners = lax.broadcasted_iota(jnp.int32, (tiles, count), 0)
    onehot = jnp.where(owners == own, 1.0, 0.0)
    at = lax.broadcasted_iota(jnp.int32, (count, count), 0)
    to = lax.broadcasted_iota(jnp.int32, (count, count), 1)
    before = jnp.where(at < to, 1.0, 0.0).astype(jnp.bfloat16)
    earlier = dot(onehot.astype(jnp.bfloat16), before, ((1,), (0,)))
    rank = jnp.sum(onehot * earlier, axis=0, keepdims=True)
    chip_here = lax.broadcasted_iota(jnp.int32, (chips, count), 0) == (own >> 1)
    even = (own & 1) == 0
    picks = []
    for r in range(CAP):
        hit = jnp.where(chip_here & (rank == float(r)), 1.0, 0.0)
        picks.append(jnp.concatenate([jnp.where(even, hit, 0.0), jnp.where(even, 0.0, hit)], axis=1))
    pick = jnp.concatenate(picks, axis=0).astype(jnp.bfloat16)
    inv = inv_ref[...]
    pad_ref[...] = jnp.zeros_like(pad_ref)
    pad_ref[0:CHAN, :] = inv
    pad_ref[FULL : FULL + CHAN, :] = inv * inno_ref[...]
    zero = jnp.zeros((2 * WIN, count), jnp.float32)
    for core in range(2):
        at = LOW * core
        both = jnp.concatenate([pad_ref[at : at + WIN, :], pad_ref[FULL + at : FULL + at + WIN, :]], axis=0)
        block = jnp.concatenate(
            [jnp.concatenate([both, zero], axis=1), jnp.concatenate([zero, both], axis=1)], axis=0
        )
        first, rest = block.astype(jnp.bfloat16), block
        rest = rest - first.astype(jnp.float32)
        second, third = split(rest)
        total = dot(pick, first, ((1,), (1,)))
        total = total + dot(pick, second, ((1,), (1,)))
        total = total + dot(pick, third, ((1,), (1,)))
        for r in range(CAP):
            out_ref[pl.ds(core * CAP + r, chips, stride=2 * CAP), :] = total[r * chips : (r + 1) * chips]


def adjoint(misfits, high_ref, low_ref, store):
    for tile in range(2):
        high, low = split(misfits[tile])
        both = jnp.concatenate([high, low], axis=0)
        wide = dot(both, high_ref[tile], ((1,), (1,)))
        flat = wide[:WIN] + wide[WIN:] + dot(high, low_ref[tile], ((1,), (1,)))
        for r in range(CY):
            store(tile * CY + r, flat[:, r * COLS : (r + 1) * COLS])


def seed_body(core_ref, mine_ref, theirs_ref, table_ref, rec_ref, *outs):
    d_ref, high_ref, low_ref, weight_ref, g_ref, up_ref, down_ref = outs
    core = core_ref[0]
    slots = table_ref.shape[1]
    base = CY * WIN
    other = jnp.concatenate(
        [theirs_ref[base + 8 * part : base + 8 * part + 8, :] for part in range(slots // COLS)], axis=1
    )
    here = table_ref[...]
    columns = lax.broadcasted_iota(jnp.int32, (COLS, slots), 0)
    slot_t = rec_ref[...].T
    targets = []
    for tile in range(2):
        first = core == tile
        table = jnp.where(first, here, other)
        cell = table[0:1].astype(jnp.int32)
        row = jnp.zeros_like(cell)
        for edge in range(1, CY - 1):
            row = row + jnp.where(cell >= edge * (COLS - 1), 1, 0)
        col = cell - row * (COLS - 1)
        at_col, at_next = col == columns, col + 1 == columns
        for r in range(CY):
            lower, upper = row == r, row == r - 1
            west = jnp.where(lower, table[1:2], 0.0) + jnp.where(upper, table[3:4], 0.0)
            east = jnp.where(lower, table[2:3], 0.0) + jnp.where(upper, table[4:5], 0.0)
            matrix = jnp.where(at_col, west, 0.0) + jnp.where(at_next, east, 0.0)
            high, low = split(matrix)
            high_ref[tile, r * COLS : (r + 1) * COLS, :] = high
            low_ref[tile, r * COLS : (r + 1) * COLS, :] = low
            d_ref[tile * CY + r] = jnp.where(first, mine_ref[r], theirs_ref[r * WIN : (r + 1) * WIN, :])
        weight_ref[tile] = slot_t[tile * 2 * WIN : tile * 2 * WIN + WIN]
        targets.append(slot_t[tile * 2 * WIN + WIN : (tile + 1) * 2 * WIN])

    def store(row, value):
        g_ref[row] = jnp.sqrt(d_ref[row]) * value

    adjoint(targets, high_ref, low_ref, store)
    up_ref[0:FAR] = g_ref[0:FAR]
    up_ref[FAR : 2 * FAR] = d_ref[0:FAR]
    down_ref[0:FAR] = g_ref[ROWS - FAR : ROWS]
    down_ref[FAR : 2 * FAR] = d_ref[ROWS - FAR : ROWS]


def places(halo):
    each = COLS // halo
    rows = range(1, ROWS + 2 * halo - 1)
    return [(row, n // each, n % each) for n, row in enumerate(rows)], -(-len(rows) // each)


def strips_body(halo, kinds, *refs):
    heres, (south_ref, north_ref, west_ref, east_ref) = refs[:kinds], refs[kinds:]
    spots, tiles = places(halo)
    lane = lax.broadcasted_iota(jnp.int32, (WIN, COLS), 1)
    for kind in range(kinds):
        for tile in range(tiles):
            west = jnp.zeros((WIN, COLS), jnp.float32)
            east = jnp.zeros((WIN, COLS), jnp.float32)
            for row, own_tile, q in spots:
                if own_tile != tile:
                    continue
                if row < halo:
                    line = south_ref[kind * halo + row]
                elif row < halo + ROWS:
                    line = heres[kind][row - halo]
                else:
                    line = north_ref[kind * halo + row - halo - ROWS]
                inside = (lane >= halo * q) & (lane < halo * q + halo)
                west = jnp.where(inside, pltpu.roll(line, halo * q, 1) if q else line, west)
                east = jnp.where(inside, pltpu.roll(line, (halo * q + halo) % COLS, 1), east)
            west_ref[kind * tiles + tile] = west
            east_ref[kind * tiles + tile] = east


def extend(dst, halo, offset, kind, here_ref, south_ref, north_ref, east_ref, west_ref):
    spots, tiles = places(halo)
    where_of = {row: (tile, q) for row, tile, q in spots}
    lane = lax.broadcasted_iota(jnp.int32, (WIN, COLS), 1)
    for row in range(ROWS + 2 * halo):
        if row < halo:
            line = south_ref[kind * halo + row]
        elif row < halo + ROWS:
            line = here_ref[row - halo]
        else:
            line = north_ref[kind * halo + row - halo - ROWS]
        dst[offset + row, :, 0:COLS] = line
        beyond = jnp.zeros((WIN, COLS), jnp.float32)
        if row in where_of:
            tile, q = where_of[row]
            right, left = east_ref[kind * tiles + tile], west_ref[kind * tiles + tile]
            right = pltpu.roll(right, COLS - halo * q, 1) if q else right
            left = pltpu.roll(left, COLS - halo - halo * q, 1)
            beyond = jnp.where(lane < halo, right, jnp.where(lane >= COLS - halo, left, 0.0))
        dst[offset + row, :, COLS:] = beyond


def sweep(src, dst, d_ref, low, high):
    lane = lax.broadcasted_iota(jnp.int32, (WIN, COLS), 1)
    last, first = lane == COLS - 1, lane == 0

    def body(row, carry):
        before, now = carry
        after = src[row + 1]
        a, b = now[:, :COLS], now[:, COLS:]
        east_a, east_b = pltpu.roll(a, COLS - 1, 1), pltpu.roll(b, COLS - 1, 1)
        west_a, west_b = pltpu.roll(a, 1, 1), pltpu.roll(b, 1, 1)
        beside_a = jnp.where(last, east_b, east_a) + jnp.where(first, west_b, west_a)
        beside_b = jnp.where(last, east_a, east_b) + jnp.where(first, west_a, west_b)
        beside = jnp.concatenate([beside_a, beside_b], axis=1)
        dst[row] = now + d_ref[row] * (before + after + beside - 4.0 * now)
        return now, after

    carry = (src[low - 1], src[low])
    for row in range(low, high):
        carry = body(row, carry)


def unscale(value, d):
    return jnp.where(d > 0.0, value * lax.rsqrt(jnp.where(d > 0.0, d, 1.0)), 0.0)


def largest(value):
    top = jnp.max(jnp.max(jnp.abs(value), axis=1, keepdims=True), axis=0, keepdims=True)
    return jnp.maximum(top, 1e-30)


def whole_sum(value):
    return jnp.sum(jnp.sum(value, axis=1, keepdims=True), axis=0, keepdims=True)


def pair_body(later, *refs):
    refs = list(refs)
    core_ref = refs.pop(0)
    here_ref, south_ref, north_ref, east_ref, west_ref = refs[:5]
    refs = refs[5:]
    if later:
        wide_d, high_ref, low_ref, weight_ref, q_in, u_in = refs[:6]
        q_ref, up_ref, down_ref, g_ref, stats_ref, first_ref, second_ref = refs[6:]
    else:
        d_ref, high_ref, low_ref, weight_ref = refs[:4]
        q_ref, u_ref, wide_d, up_ref, down_ref, g_ref, first_ref, second_ref = refs[4:]
        extend(wide_d, FAR, 0, 1, d_ref, south_ref, north_ref, east_ref, west_ref)
    extend(first_ref, FAR, 0, 0, here_ref, south_ref, north_ref, east_ref, west_ref)
    src, dst = first_ref, second_ref
    total = ROWS + 2 * FAR
    halo = STEPS if later else FAR
    rows = []
    for step in range(1, FAR + 1):
        sweep(src, dst, wide_d, step, total - step)
        src, dst = dst, src
        if step == STEPS:
            for r in range(ROWS):
                value = unscale(src[FAR + r, :, 0:COLS], wide_d[FAR + r, :, 0:COLS])
                q_ref[r] = q_in[r] + value if later else value
    for r in range(ROWS):
        value = unscale(src[FAR + r, :, 0:COLS], wide_d[FAR + r, :, 0:COLS])
        if later:
            value = value + u_in[r]
        else:
            u_ref[r] = value
        rows.append(value)
    misfits, samples = [], []
    for tile in range(2):
        flat = jnp.concatenate(rows[tile * CY : (tile + 1) * CY], axis=1)
        high, low = split(flat)
        both = dot(jnp.concatenate([high, low], axis=0), high_ref[tile], ((1,), (0,)))
        value = both[:WIN] + both[WIN:] + dot(high, low_ref[tile], ((1,), (0,)))
        samples.append(value)
        misfits.append(weight_ref[tile] * value)

    def store(row, value):
        g_ref[row] = jnp.sqrt(wide_d[FAR + row, :, 0:COLS]) * value

    adjoint(misfits, high_ref, low_ref, store)
    up_ref[...] = g_ref[0:halo]
    down_ref[...] = g_ref[ROWS - halo : ROWS]
    if later:
        sub = lax.broadcasted_iota(jnp.int32, (WIN, 1), 0)
        keep = jnp.where((sub < LOW) | (core_ref[0] == 1), 1.0, 0.0)
        top0 = jnp.zeros((WIN, COLS), jnp.float32)
        top1 = jnp.zeros((WIN, COLS), jnp.float32)
        for r in range(ROWS):
            top0 = jnp.maximum(top0, jnp.abs(q_in[r]))
            top1 = jnp.maximum(top1, jnp.abs(q_ref[r]))
        t0, t1 = largest(top0), largest(top1)
        v1 = jnp.maximum(largest(samples[0]), largest(samples[1]))
        i0, i1, iv = 1.0 / t0, 1.0 / t1, 1.0 / v1
        sums = [jnp.zeros((WIN, COLS), jnp.float32) for _ in range(3)]
        for r in range(ROWS):
            a, b = q_in[r] * i0, q_ref[r] * i1
            sums = [sums[0] + a * a, sums[1] + a * b, sums[2] + b * b]
        values = [whole_sum(s * keep) for s in sums]
        quad = sum(weight_ref[tile] * (samples[tile] * iv) * (samples[tile] * iv) for tile in range(2))
        values += [whole_sum(quad * keep), t0, t1, v1]
        stats_ref[...] = jnp.broadcast_to(as_row(values)[None], stats_ref.shape)


def as_row(values):
    lane = lax.broadcasted_iota(jnp.int32, (1, COLS), 1)
    row = jnp.zeros((1, COLS), jnp.float32)
    for n, value in enumerate(values):
        row = jnp.where(lane == n, value, row)
    return row


def merged(block):
    part = [block[:, n : n + 1] for n in range(7)]
    tops = [jnp.max(part[n], axis=0, keepdims=True) for n in (4, 5, 6)]
    r0, r1, rv = (part[4 + n] / tops[n] for n in range(3))
    values = [part[0] * r0 * r0, part[1] * r0 * r1, part[2] * r1 * r1, part[3] * rv * rv]
    return [jnp.sum(value, axis=0, keepdims=True) for value in values] + tops


def merge_body(in_ref, out_ref):
    out_ref[...] = jnp.broadcast_to(as_row(merged(in_ref[:, 0, :]))[None], out_ref.shape)


def last_body(core_ref, here_ref, south_ref, north_ref, east_ref, west_ref, wide_d, q0_ref, q1_ref, *outs):
    mine_ref, mate_ref, first_ref, second_ref, near_d, q2_ref = outs
    core = core_ref[0]
    total = ROWS + 2 * STEPS
    extend(first_ref, STEPS, 0, 0, here_ref, south_ref, north_ref, east_ref, west_ref)
    for row in range(total):
        near_d[row] = wide_d[row + FAR - STEPS]
    src, dst = first_ref, second_ref
    for step in range(1, STEPS + 1):
        sweep(src, dst, near_d, step, total - step)
        src, dst = dst, src
    for r in range(ROWS):
        d = near_d[STEPS + r, :, 0:COLS]
        q2_ref[r] = q1_ref[r] + unscale(src[STEPS + r, :, 0:COLS], d)
    for n, q in enumerate((q0_ref, q1_ref, q2_ref)):
        mine_ref[n * CY : (n + 1) * CY] = q[pl.ds(core * CY, CY)]
        mate_ref[n * CY : (n + 1) * CY] = q[pl.ds((1 - core) * CY, CY)]


def final_body(core_ref, mine_ref, theirs_ref, stats_ref, control_ref, residual_ref, c_ref, r_ref):
    core = core_ref[0]
    m00, m01, m11, s11, t0, t1, v1 = merged(stats_ref[:, 0, :])
    ratio = t1 / t0
    scaled = m00 / m01
    alpha0 = scaled / ratio
    norm1 = m00 - 2.0 * scaled * m01 + scaled * scaled * m11
    beta = norm1 / m00
    lift = 1.0 + beta
    relative = v1 / t1
    curve = lift * lift * ratio * m01 - 2.0 * lift * scaled * ratio * m11
    curve = curve + scaled * scaled * (m11 + relative * relative * s11)
    alpha1 = norm1 / curve
    one = alpha0 + alpha1 * lift
    two = alpha1 * alpha0
    for ref, owner in ((mine_ref, core), (theirs_ref, 1 - core)):
        for r in range(CY):
            q0, q1, q2 = ref[r], ref[CY + r], ref[2 * CY + r]
            at = LOW * CY * owner + r
            c_ref[pl.ds(at, WIN, stride=CY), :] = one * q0 - two * q1
            r_ref[pl.ds(at, WIN, stride=CY), :] = q0 - one * q1 + two * q2
    control_ref[...] = c_ref[0 : CHAN * CY, :].reshape(CHAN, CY, COLS)
    residual_ref[...] = r_ref[0 : CHAN * CY, :].reshape(CHAN, CY, COLS)


def on_device(
    diffusivity, land_mask, innovation, inverse_variance, owner_ids, cell_index, corner_weights
):
    count_x, count_y = lax.axis_size("gx"), lax.axis_size("gy")
    slots = count_y * CAP
    core = (lax.axis_index("gy") % 2).astype(jnp.int32).reshape(1)
    count = owner_ids.shape[0]

    def along_y(value, by):
        pairs = [(i, i + by) for i in range(count_y) if 0 <= i + by < count_y]
        return lax.ppermute(value, "gy", pairs)

    def along_x(value, by):
        return lax.ppermute(value, "gx", [(i, (i + by) % count_x) for i in range(count_x)])

    def across(value):
        return lax.ppermute(value, "gy", [(i, i ^ 1) for i in range(count_y)])

    def exchange(heres, up, down, halo, *after):
        kinds = len(heres)
        tiles = places(halo)[1]
        south, north = along_y(down, 2), along_y(up, -2)
        pack = call(functools.partial(strips_body, halo, kinds), [f32(kinds * tiles, WIN, COLS)] * 2, 10**6)
        west, east = pack(*heres, south, north)
        west, east, *after = lax.optimization_barrier((west, east, *after))
        return south, north, along_x(west, -1), along_x(east, 1), *after

    field = f32(ROWS, WIN, COLS)
    ins = [
        owner_ids.reshape(1, count), inverse_variance, innovation, diffusivity, land_mask, cell_index, corner_weights
    ]
    space = [pltpu.VMEM(x.shape, x.dtype) for x in ins]
    space += [pltpu.VMEM((2 * FULL, count), jnp.float32), pltpu.VMEM((FULL * CY, COLS), jnp.float32)]
    chunks, mine, mate, table = call(
        first_body,
        [f32(slots, COLS), f32(CY, WIN, COLS), f32(CY * WIN + 8 * (slots // COLS), COLS), f32(8, slots)],
        10**7,
        space + [pltpu.SemaphoreType.DMA((len(ins),))],
        1,
        pltpu.HBM,
    )(core, *(pltpu.with_memory_space_constraint(x, pltpu.HBM) for x in ins))
    theirs = across(mate)
    received = lax.all_to_all(chunks, "gy", split_axis=0, concat_axis=0, tiled=True)
    matrix = jax.ShapeDtypeStruct((2, CY * COLS, slots), jnp.bfloat16)
    both = f32(2 * FAR, WIN, COLS)
    d, high, low, weights, g, up, down = call(
        seed_body, [field, matrix, matrix, f32(2, WIN, slots), field, both, both], 10**8, (), 1
    )(core, mine, theirs, table, received)
    wide = (ROWS + 2 * FAR, WIN, 2 * COLS)
    space = [pltpu.VMEM(wide, jnp.float32)] * 2
    south, north, east, west = exchange([g, d], up, down, FAR)
    q0, u0, wide_d, up, down, g = call(
        functools.partial(pair_body, False),
        [field, field, f32(*wide), f32(FAR, WIN, COLS), f32(FAR, WIN, COLS), field],
        2 * 10**8,
        space,
        1,
    )(core, g, south, north, east, west, d, high, low, weights)
    south, north, east, west = exchange([g], up, down, FAR)
    q1, up, down, g, stats = call(
        functools.partial(pair_body, True),
        [field, f32(STEPS, WIN, COLS), f32(STEPS, WIN, COLS), field, f32(count_y, 2, COLS)],
        2 * 10**8,
        space,
        1,
    )(core, g, south, north, east, west, wide_d, high, low, weights, q0, u0)
    stats = lax.all_to_all(stats, "gy", split_axis=0, concat_axis=0, tiled=True)
    (stats,) = call(merge_body, [f32(count_x, 2, COLS)], 10**5)(stats)
    south, north, east, west, stats = exchange([g], up, down, STEPS, stats)
    stats = lax.all_to_all(stats, "gx", split_axis=0, concat_axis=0, tiled=True)
    near = (ROWS + 2 * STEPS, WIN, 2 * COLS)
    mine, mate = call(
        last_body,
        [f32(3 * CY, WIN, COLS)] * 2,
        10**8,
        [pltpu.VMEM(near, jnp.float32)] * 3 + [pltpu.VMEM((ROWS, WIN, COLS), jnp.float32)],
        1,
    )(core, g, south, north, east, west, wide_d, q0, q1)
    mate, stats = lax.optimization_barrier((mate, stats))
    theirs = across(mate)
    out = f32(CHAN, CY, COLS)
    return call(
        final_body, [out, out], 10**6, [pltpu.VMEM((FULL * CY, COLS), jnp.float32)] * 2, 1
    )(core, mine, theirs, stats)


def solution(mesh):
    return jax.shard_map(
        on_device,
        mesh=mesh,
        in_specs=(
            P(None, "gy", "gx"),
            P("gy", "gx"),
            P(None, ("gx", "gy")),
            P(None, ("gx", "gy")),
            P(("gx", "gy"), None),
            P(("gx", "gy"), None),
            P(None, ("gx", "gy"), None),
        ),
        out_specs=(P(None, "gy", "gx"), P(None, "gy", "gx")),
        check_vma=False,
    )
```

```python
import functools

import jax
import jax.numpy as jnp
from jax import lax
from jax.experimental import pallas as pl
from jax.experimental.pallas import tpu as pltpu
from jax.sharding import PartitionSpec as P

CAP = 4
STEPS = 5
CHAN = 50
WIN = 32
LOW = 24
FULL = 56
COLS = 128
CY = 8
ROWS = 2 * CY
FAR = 2 * STEPS


def call(body, outs, flops, scratch=(), scalars=0, source=pltpu.VMEM):
    def run(*args):
        size = sum(a.size * a.dtype.itemsize for a in args) + sum(o.size * o.dtype.itemsize for o in outs)
        specs = [pl.BlockSpec(memory_space=pltpu.SMEM)] * scalars
        specs += [pl.BlockSpec(memory_space=source)] * (len(args) - scalars)
        return pl.pallas_call(
            body,
            out_shape=tuple(outs),
            in_specs=specs,
            out_specs=tuple(pl.BlockSpec(memory_space=pltpu.VMEM) for _ in outs),
            scratch_shapes=list(scratch),
            compiler_params=pltpu.CompilerParams(vmem_limit_bytes=16 * 1024 * 1024),
            cost_estimate=pl.CostEstimate(flops=flops, bytes_accessed=size, transcendentals=0),
        )(*args)

    return run


def f32(*shape):
    return jax.ShapeDtypeStruct(shape, jnp.float32)


def split(value):
    high = value.astype(jnp.bfloat16)
    return high, (value - high.astype(jnp.float32)).astype(jnp.bfloat16)


def dot(a, b, dims):
    return lax.dot_general(a, b, (dims, ((), ())), preferred_element_type=jnp.float32)


def first_body(core_ref, *refs):
    ins, (chunk_ref, mine_ref, mate_ref, table_ref), space = refs[:7], refs[7:11], refs[11:]
    held, pad_ref, field_ref, sems = space[:7], space[7], space[8], space[9]
    copies = [pltpu.make_async_copy(ins[n], held[n], sems.at[n]) for n in range(7)]
    for copy in copies:
        copy.start()
    own_ref, inv_ref, inno_ref, diff_ref, mask_ref, cell_ref, corner_ref = held
    for copy in copies:
        copy.wait()
    route(own_ref, inv_ref, inno_ref, chunk_ref, pad_ref)
    core = core_ref[0]
    slots = cell_ref.shape[1]
    masked = diff_ref[...] * mask_ref[...].astype(jnp.float32)[None]
    field_ref[0 : CHAN * CY, :] = masked.reshape(CHAN * CY, COLS)
    field_ref[CHAN * CY :, :] = jnp.zeros((FULL * CY - CHAN * CY, COLS), jnp.float32)
    for r in range(CY):
        at = LOW * CY * core + r
        mine_ref[r] = field_ref[pl.ds(at, WIN, stride=CY), :]
        at = LOW * CY * (1 - core) + r
        mate_ref[r * WIN : (r + 1) * WIN, :] = field_ref[pl.ds(at, WIN, stride=CY), :]
    base = CY * WIN
    rows = [cell_ref[...].astype(jnp.float32)] + [corner_ref[n] for n in range(4)]
    table = jnp.concatenate(rows + [jnp.zeros((3, slots), jnp.float32)], axis=0)
    table_ref[...] = table
    for part in range(slots // COLS):
        mate_ref[base + 8 * part : base + 8 * part + 8, :] = table[:, part * COLS : (part + 1) * COLS]


def route(own_ref, inv_ref, inno_ref, out_ref, pad_ref):
    count = own_ref.shape[1]
    tiles = out_ref.shape[0] // CAP
    chips = tiles // 2
    own = own_ref[...]
    owners = lax.broadcasted_iota(jnp.int32, (tiles, count), 0)
    onehot = jnp.where(owners == own, 1.0, 0.0)
    at = lax.broadcasted_iota(jnp.int32, (count, count), 0)
    to = lax.broadcasted_iota(jnp.int32, (count, count), 1)
    before = jnp.where(at < to, 1.0, 0.0).astype(jnp.bfloat16)
    earlier = dot(onehot.astype(jnp.bfloat16), before, ((1,), (0,)))
    rank = jnp.sum(onehot * earlier, axis=0, keepdims=True)
    chip_here = lax.broadcasted_iota(jnp.int32, (chips, count), 0) == (own >> 1)
    even = (own & 1) == 0
    picks = []
    for r in range(CAP):
        hit = jnp.where(chip_here & (rank == float(r)), 1.0, 0.0)
        picks.append(jnp.concatenate([jnp.where(even, hit, 0.0), jnp.where(even, 0.0, hit)], axis=1))
    pick = jnp.concatenate(picks, axis=0).astype(jnp.bfloat16)
    inv = inv_ref[...]
    pad_ref[...] = jnp.zeros_like(pad_ref)
    pad_ref[0:CHAN, :] = inv
    pad_ref[FULL : FULL + CHAN, :] = inv * inno_ref[...]
    zero = jnp.zeros((2 * WIN, count), jnp.float32)
    for core in range(2):
        at = LOW * core
        both = jnp.concatenate([pad_ref[at : at + WIN, :], pad_ref[FULL + at : FULL + at + WIN, :]], axis=0)
        block = jnp.concatenate(
            [jnp.concatenate([both, zero], axis=1), jnp.concatenate([zero, both], axis=1)], axis=0
        )
        first, rest = block.astype(jnp.bfloat16), block
        rest = rest - first.astype(jnp.float32)
        second, third = split(rest)
        total = dot(pick, first, ((1,), (1,)))
        total = total + dot(pick, second, ((1,), (1,)))
        total = total + dot(pick, third, ((1,), (1,)))
        for r in range(CAP):
            out_ref[pl.ds(core * CAP + r, chips, stride=2 * CAP), :] = total[r * chips : (r + 1) * chips]


def adjoint(misfits, high_ref, low_ref, store):
    for tile in range(2):
        high, low = split(misfits[tile])
        both = jnp.concatenate([high, low], axis=0)
        wide = dot(both, high_ref[tile], ((1,), (1,)))
        flat = wide[:WIN] + wide[WIN:] + dot(high, low_ref[tile], ((1,), (1,)))
        for r in range(CY):
            store(tile * CY + r, flat[:, r * COLS : (r + 1) * COLS])


def seed_body(core_ref, mine_ref, theirs_ref, table_ref, rec_ref, *outs):
    d_ref, high_ref, low_ref, weight_ref, g_ref, up_ref, down_ref = outs
    core = core_ref[0]
    slots = table_ref.shape[1]
    base = CY * WIN
    other = jnp.concatenate(
        [theirs_ref[base + 8 * part : base + 8 * part + 8, :] for part in range(slots // COLS)], axis=1
    )
    here = table_ref[...]
    columns = lax.broadcasted_iota(jnp.int32, (COLS, slots), 0)
    slot_t = rec_ref[...].T
    targets = []
    for tile in range(2):
        first = core == tile
        table = jnp.where(first, here, other)
        cell = table[0:1].astype(jnp.int32)
        row = jnp.zeros_like(cell)
        for edge in range(1, CY - 1):
            row = row + jnp.where(cell >= edge * (COLS - 1), 1, 0)
        col = cell - row * (COLS - 1)
        at_col, at_next = col == columns, col + 1 == columns
        for r in range(CY):
            lower, upper = row == r, row == r - 1
            west = jnp.where(lower, table[1:2], 0.0) + jnp.where(upper, table[3:4], 0.0)
            east = jnp.where(lower, table[2:3], 0.0) + jnp.where(upper, table[4:5], 0.0)
            matrix = jnp.where(at_col, west, 0.0) + jnp.where(at_next, east, 0.0)
            high, low = split(matrix)
            high_ref[tile, r * COLS : (r + 1) * COLS, :] = high
            low_ref[tile, r * COLS : (r + 1) * COLS, :] = low
            d_ref[tile * CY + r] = jnp.where(first, mine_ref[r], theirs_ref[r * WIN : (r + 1) * WIN, :])
        weight_ref[tile] = slot_t[tile * 2 * WIN : tile * 2 * WIN + WIN]
        targets.append(slot_t[tile * 2 * WIN + WIN : (tile + 1) * 2 * WIN])

    def store(row, value):
        g_ref[row] = jnp.sqrt(d_ref[row]) * value

    adjoint(targets, high_ref, low_ref, store)
    up_ref[0:FAR] = g_ref[0:FAR]
    up_ref[FAR : 2 * FAR] = d_ref[0:FAR]
    down_ref[0:FAR] = g_ref[ROWS - FAR : ROWS]
    down_ref[FAR : 2 * FAR] = d_ref[ROWS - FAR : ROWS]


def places(halo):
    each = COLS // halo
    rows = range(1, ROWS + 2 * halo - 1)
    return [(row, n // each, n % each) for n, row in enumerate(rows)], -(-len(rows) // each)


def strips_body(halo, kinds, *refs):
    heres, (south_ref, north_ref, west_ref, east_ref) = refs[:kinds], refs[kinds:]
    spots, tiles = places(halo)
    lane = lax.broadcasted_iota(jnp.int32, (WIN, COLS), 1)
    for kind in range(kinds):
        for tile in range(tiles):
            west = jnp.zeros((WIN, COLS), jnp.float32)
            east = jnp.zeros((WIN, COLS), jnp.float32)
            for row, own_tile, q in spots:
                if own_tile != tile:
                    continue
                if row < halo:
                    line = south_ref[kind * halo + row]
                elif row < halo + ROWS:
                    line = heres[kind][row - halo]
                else:
                    line = north_ref[kind * halo + row - halo - ROWS]
                inside = (lane >= halo * q) & (lane < halo * q + halo)
                west = jnp.where(inside, pltpu.roll(line, halo * q, 1) if q else line, west)
                east = jnp.where(inside, pltpu.roll(line, (halo * q + halo) % COLS, 1), east)
            west_ref[kind * tiles + tile] = west
            east_ref[kind * tiles + tile] = east


def extend(dst, halo, offset, kind, here_ref, south_ref, north_ref, east_ref, west_ref):
    spots, tiles = places(halo)
    where_of = {row: (tile, q) for row, tile, q in spots}
    lane = lax.broadcasted_iota(jnp.int32, (WIN, COLS), 1)
    for row in range(ROWS + 2 * halo):
        if row < halo:
            line = south_ref[kind * halo + row]
        elif row < halo + ROWS:
            line = here_ref[row - halo]
        else:
            line = north_ref[kind * halo + row - halo - ROWS]
        dst[offset + row, :, 0:COLS] = line
        beyond = jnp.zeros((WIN, COLS), jnp.float32)
        if row in where_of:
            tile, q = where_of[row]
            right, left = east_ref[kind * tiles + tile], west_ref[kind * tiles + tile]
            right = pltpu.roll(right, COLS - halo * q, 1) if q else right
            left = pltpu.roll(left, COLS - halo - halo * q, 1)
            beyond = jnp.where(lane < halo, right, jnp.where(lane >= COLS - halo, left, 0.0))
        dst[offset + row, :, COLS:] = beyond


def sweep(src, dst, d_ref, low, high):
    lane = lax.broadcasted_iota(jnp.int32, (WIN, COLS), 1)
    last, first = lane == COLS - 1, lane == 0

    def body(row, carry):
        before, now = carry
        after = src[row + 1]
        a, b = now[:, :COLS], now[:, COLS:]
        east_a, east_b = pltpu.roll(a, COLS - 1, 1), pltpu.roll(b, COLS - 1, 1)
        west_a, west_b = pltpu.roll(a, 1, 1), pltpu.roll(b, 1, 1)
        beside_a = jnp.where(last, east_b, east_a) + jnp.where(first, west_b, west_a)
        beside_b = jnp.where(last, east_a, east_b) + jnp.where(first, west_a, west_b)
        beside = jnp.concatenate([beside_a, beside_b], axis=1)
        dst[row] = now + d_ref[row] * (before + after + beside - 4.0 * now)
        return now, after

    carry = (src[low - 1], src[low])
    for row in range(low, high):
        carry = body(row, carry)


def unscale(value, d):
    return jnp.where(d > 0.0, value * lax.rsqrt(jnp.where(d > 0.0, d, 1.0)), 0.0)


def largest(value):
    top = jnp.max(jnp.max(jnp.abs(value), axis=1, keepdims=True), axis=0, keepdims=True)
    return jnp.maximum(top, 1e-30)


def whole_sum(value):
    return jnp.sum(jnp.sum(value, axis=1, keepdims=True), axis=0, keepdims=True)


def pair_body(later, *refs):
    refs = list(refs)
    core_ref = refs.pop(0)
    here_ref, south_ref, north_ref, east_ref, west_ref = refs[:5]
    refs = refs[5:]
    if later:
        wide_d, high_ref, low_ref, weight_ref, q_in, u_in = refs[:6]
        q_ref, up_ref, down_ref, g_ref, stats_ref, first_ref, second_ref = refs[6:]
    else:
        d_ref, high_ref, low_ref, weight_ref = refs[:4]
        q_ref, u_ref, wide_d, up_ref, down_ref, g_ref, first_ref, second_ref = refs[4:]
        extend(wide_d, FAR, 0, 1, d_ref, south_ref, north_ref, east_ref, west_ref)
    extend(first_ref, FAR, 0, 0, here_ref, south_ref, north_ref, east_ref, west_ref)
    src, dst = first_ref, second_ref
    total = ROWS + 2 * FAR
    halo = STEPS if later else FAR
    rows = []
    for step in range(1, FAR + 1):
        sweep(src, dst, wide_d, step, total - step)
        src, dst = dst, src
        if step == STEPS:
            for r in range(ROWS):
                value = unscale(src[FAR + r, :, 0:COLS], wide_d[FAR + r, :, 0:COLS])
                q_ref[r] = q_in[r] + value if later else value
    for r in range(ROWS):
        value = unscale(src[FAR + r, :, 0:COLS], wide_d[FAR + r, :, 0:COLS])
        if later:
            value = value + u_in[r]
        else:
            u_ref[r] = value
        rows.append(value)
    misfits, samples = [], []
    for tile in range(2):
        flat = jnp.concatenate(rows[tile * CY : (tile + 1) * CY], axis=1)
        high, low = split(flat)
        both = dot(jnp.concatenate([high, low], axis=0), high_ref[tile], ((1,), (0,)))
        value = both[:WIN] + both[WIN:] + dot(high, low_ref[tile], ((1,), (0,)))
        samples.append(value)
        misfits.append(weight_ref[tile] * value)

    def store(row, value):
        g_ref[row] = jnp.sqrt(wide_d[FAR + row, :, 0:COLS]) * value

    adjoint(misfits, high_ref, low_ref, store)
    up_ref[...] = g_ref[0:halo]
    down_ref[...] = g_ref[ROWS - halo : ROWS]
    if later:
        sub = lax.broadcasted_iota(jnp.int32, (WIN, 1), 0)
        keep = jnp.where((sub < LOW) | (core_ref[0] == 1), 1.0, 0.0)
        top0 = jnp.zeros((WIN, COLS), jnp.float32)
        top1 = jnp.zeros((WIN, COLS), jnp.float32)
        for r in range(ROWS):
            top0 = jnp.maximum(top0, jnp.abs(q_in[r]))
            top1 = jnp.maximum(top1, jnp.abs(q_ref[r]))
        t0, t1 = largest(top0), largest(top1)
        v1 = jnp.maximum(largest(samples[0]), largest(samples[1]))
        i0, i1, iv = 1.0 / t0, 1.0 / t1, 1.0 / v1
        sums = [jnp.zeros((WIN, COLS), jnp.float32) for _ in range(3)]
        for r in range(ROWS):
            a, b = q_in[r] * i0, q_ref[r] * i1
            sums = [sums[0] + a * a, sums[1] + a * b, sums[2] + b * b]
        values = [whole_sum(s * keep) for s in sums]
        quad = sum(weight_ref[tile] * (samples[tile] * iv) * (samples[tile] * iv) for tile in range(2))
        values += [whole_sum(quad * keep), t0, t1, v1]
        stats_ref[...] = jnp.broadcast_to(as_row(values)[None], stats_ref.shape)


def as_row(values):
    lane = lax.broadcasted_iota(jnp.int32, (1, COLS), 1)
    row = jnp.zeros((1, COLS), jnp.float32)
    for n, value in enumerate(values):
        row = jnp.where(lane == n, value, row)
    return row


def merged(block):
    part = [block[:, n : n + 1] for n in range(7)]
    tops = [jnp.max(part[n], axis=0, keepdims=True) for n in (4, 5, 6)]
    r0, r1, rv = (part[4 + n] / tops[n] for n in range(3))
    values = [part[0] * r0 * r0, part[1] * r0 * r1, part[2] * r1 * r1, part[3] * rv * rv]
    return [jnp.sum(value, axis=0, keepdims=True) for value in values] + tops


def merge_body(in_ref, out_ref):
    out_ref[...] = jnp.broadcast_to(as_row(merged(in_ref[:, 0, :]))[None], out_ref.shape)


def last_body(core_ref, here_ref, south_ref, north_ref, east_ref, west_ref, wide_d, q0_ref, q1_ref, *outs):
    mine_ref, mate_ref, first_ref, second_ref, near_d, q2_ref = outs
    core = core_ref[0]
    total = ROWS + 2 * STEPS
    extend(first_ref, STEPS, 0, 0, here_ref, south_ref, north_ref, east_ref, west_ref)
    for row in range(total):
        near_d[row] = wide_d[row + FAR - STEPS]
    src, dst = first_ref, second_ref
    for step in range(1, STEPS + 1):
        sweep(src, dst, near_d, step, total - step)
        src, dst = dst, src
    for r in range(ROWS):
        d = near_d[STEPS + r, :, 0:COLS]
        q2_ref[r] = q1_ref[r] + unscale(src[STEPS + r, :, 0:COLS], d)
    for n, q in enumerate((q0_ref, q1_ref, q2_ref)):
        mine_ref[n * CY : (n + 1) * CY] = q[pl.ds(core * CY, CY)]
        mate_ref[n * CY : (n + 1) * CY] = q[pl.ds((1 - core) * CY, CY)]


def final_body(core_ref, mine_ref, theirs_ref, stats_ref, control_ref, residual_ref, c_ref, r_ref):
    core = core_ref[0]
    m00, m01, m11, s11, t0, t1, v1 = merged(stats_ref[:, 0, :])
    ratio = t1 / t0
    scaled = m00 / m01
    alpha0 = scaled / ratio
    norm1 = m00 - 2.0 * scaled * m01 + scaled * scaled * m11
    beta = norm1 / m00
    lift = 1.0 + beta
    relative = v1 / t1
    curve = lift * lift * ratio * m01 - 2.0 * lift * scaled * ratio * m11
    curve = curve + scaled * scaled * (m11 + relative * relative * s11)
    alpha1 = norm1 / curve
    one = alpha0 + alpha1 * lift
    two = alpha1 * alpha0
    for ref, owner in ((mine_ref, core), (theirs_ref, 1 - core)):
        for r in range(CY):
            q0, q1, q2 = ref[r], ref[CY + r], ref[2 * CY + r]
            at = LOW * CY * owner + r
            c_ref[pl.ds(at, WIN, stride=CY), :] = one * q0 - two * q1
            r_ref[pl.ds(at, WIN, stride=CY), :] = q0 - one * q1 + two * q2
    control_ref[...] = c_ref[0 : CHAN * CY, :].reshape(CHAN, CY, COLS)
    residual_ref[...] = r_ref[0 : CHAN * CY, :].reshape(CHAN, CY, COLS)


def on_device(
    diffusivity, land_mask, innovation, inverse_variance, owner_ids, cell_index, corner_weights
):
    count_x, count_y = lax.axis_size("gx"), lax.axis_size("gy")
    slots = count_y * CAP
    core = (lax.axis_index("gy") % 2).astype(jnp.int32).reshape(1)
    count = owner_ids.shape[0]

    def along_y(value, by):
        pairs = [(i, i + by) for i in range(count_y) if 0 <= i + by < count_y]
        return lax.ppermute(value, "gy", pairs)

    def along_x(value, by):
        return lax.ppermute(value, "gx", [(i, (i + by) % count_x) for i in range(count_x)])

    def across(value):
        return lax.ppermute(value, "gy", [(i, i ^ 1) for i in range(count_y)])

    def exchange(heres, up, down, halo):
        kinds = len(heres)
        tiles = places(halo)[1]
        south, north = along_y(down, 2), along_y(up, -2)
        pack = call(functools.partial(strips_body, halo, kinds), [f32(kinds * tiles, WIN, COLS)] * 2, 10**6)
        west, east = pack(*heres, south, north)
        return south, north, along_x(west, -1), along_x(east, 1)

    field = f32(ROWS, WIN, COLS)
    ins = [
        owner_ids.reshape(1, count), inverse_variance, innovation, diffusivity, land_mask, cell_index, corner_weights
    ]
    space = [pltpu.VMEM(x.shape, x.dtype) for x in ins]
    space += [pltpu.VMEM((2 * FULL, count), jnp.float32), pltpu.VMEM((FULL * CY, COLS), jnp.float32)]
    chunks, mine, mate, table = call(
        first_body,
        [f32(slots, COLS), f32(CY, WIN, COLS), f32(CY * WIN + 8 * (slots // COLS), COLS), f32(8, slots)],
        10**7,
        space + [pltpu.SemaphoreType.DMA((len(ins),))],
        1,
        pltpu.HBM,
    )(core, *(pltpu.with_memory_space_constraint(x, pltpu.HBM) for x in ins))
    theirs = across(mate)
    received = lax.all_to_all(chunks, "gy", split_axis=0, concat_axis=0, tiled=True)
    matrix = jax.ShapeDtypeStruct((2, CY * COLS, slots), jnp.bfloat16)
    both = f32(2 * FAR, WIN, COLS)
    d, high, low, weights, g, up, down = call(
        seed_body, [field, matrix, matrix, f32(2, WIN, slots), field, both, both], 10**8, (), 1
    )(core, mine, theirs, table, received)
    wide = (ROWS + 2 * FAR, WIN, 2 * COLS)
    space = [pltpu.VMEM(wide, jnp.float32)] * 2
    south, north, east, west = exchange([g, d], up, down, FAR)
    q0, u0, wide_d, up, down, g = call(
        functools.partial(pair_body, False),
        [field, field, f32(*wide), f32(FAR, WIN, COLS), f32(FAR, WIN, COLS), field],
        2 * 10**8,
        space,
        1,
    )(core, g, south, north, east, west, d, high, low, weights)
    south, north, east, west = exchange([g], up, down, FAR)
    q1, up, down, g, stats = call(
        functools.partial(pair_body, True),
        [field, f32(STEPS, WIN, COLS), f32(STEPS, WIN, COLS), field, f32(count_y, 1, COLS)],
        2 * 10**8,
        space,
        1,
    )(core, g, south, north, east, west, wide_d, high, low, weights, q0, u0)
    stats = lax.all_to_all(stats, "gy", split_axis=0, concat_axis=0, tiled=True)
    (stats,) = call(merge_body, [f32(count_x, 1, COLS)], 10**5)(stats)
    south, north, east, west = exchange([g], up, down, STEPS)
    stats = lax.all_to_all(stats, "gx", split_axis=0, concat_axis=0, tiled=True)
    near = (ROWS + 2 * STEPS, WIN, 2 * COLS)
    mine, mate = call(
        last_body,
        [f32(3 * CY, WIN, COLS)] * 2,
        10**8,
        [pltpu.VMEM(near, jnp.float32)] * 3 + [pltpu.VMEM((ROWS, WIN, COLS), jnp.float32)],
        1,
    )(core, g, south, north, east, west, wide_d, q0, q1)
    mate, stats = lax.optimization_barrier((mate, stats))
    theirs = across(mate)
    out = f32(CHAN, CY, COLS)
    return call(
        final_body, [out, out], 10**6, [pltpu.VMEM((FULL * CY, COLS), jnp.float32)] * 2, 1
    )(core, mine, theirs, stats)


def solution(mesh):
    return jax.shard_map(
        on_device,
        mesh=mesh,
        in_specs=(
            P(None, "gy", "gx"),
            P("gy", "gx"),
            P(None, ("gx", "gy")),
            P(None, ("gx", "gy")),
            P(("gx", "gy"), None),
            P(("gx", "gy"), None),
            P(None, ("gx", "gy"), None),
        ),
        out_specs=(P(None, "gy", "gx"), P(None, "gy", "gx")),
        check_vma=False,
    )
```

```python
import functools

import jax
import jax.numpy as jnp
from jax import lax
from jax.experimental import pallas as pl
from jax.experimental.pallas import tpu as pltpu
from jax.sharding import PartitionSpec as P

CAP = 4
STEPS = 5
CHAN = 50
WIN = 32
LOW = 24
FULL = 56
COLS = 128
CY = 8
ROWS = 2 * CY
FAR = 2 * STEPS


def call(body, outs, flops, scratch=(), scalars=0, source=pltpu.VMEM):
    def run(*args):
        size = sum(a.size * a.dtype.itemsize for a in args) + sum(o.size * o.dtype.itemsize for o in outs)
        specs = [pl.BlockSpec(memory_space=pltpu.SMEM)] * scalars
        specs += [pl.BlockSpec(memory_space=source)] * (len(args) - scalars)
        return pl.pallas_call(
            body,
            out_shape=tuple(outs),
            in_specs=specs,
            out_specs=tuple(pl.BlockSpec(memory_space=pltpu.VMEM) for _ in outs),
            scratch_shapes=list(scratch),
            compiler_params=pltpu.CompilerParams(vmem_limit_bytes=16 * 1024 * 1024),
            cost_estimate=pl.CostEstimate(flops=flops, bytes_accessed=size, transcendentals=0),
        )(*args)

    return run


def f32(*shape):
    return jax.ShapeDtypeStruct(shape, jnp.float32)


def split(value):
    high = value.astype(jnp.bfloat16)
    return high, (value - high.astype(jnp.float32)).astype(jnp.bfloat16)


def dot(a, b, dims):
    return lax.dot_general(a, b, (dims, ((), ())), preferred_element_type=jnp.float32)


def first_body(core_ref, *refs):
    ins, (chunk_ref, mine_ref, mate_ref, table_ref), space = refs[:7], refs[7:11], refs[11:]
    held, pad_ref, field_ref, sems = space[:7], space[7], space[8], space[9]
    copies = [pltpu.make_async_copy(ins[n], held[n], sems.at[n]) for n in range(7)]
    for copy in copies:
        copy.start()
    own_ref, inv_ref, inno_ref, diff_ref, mask_ref, cell_ref, corner_ref = held
    for copy in copies:
        copy.wait()
    route(own_ref, inv_ref, inno_ref, chunk_ref, pad_ref)
    core = core_ref[0]
    slots = cell_ref.shape[1]
    masked = diff_ref[...] * mask_ref[...].astype(jnp.float32)[None]
    field_ref[0 : CHAN * CY, :] = masked.reshape(CHAN * CY, COLS)
    field_ref[CHAN * CY :, :] = jnp.zeros((FULL * CY - CHAN * CY, COLS), jnp.float32)
    for r in range(CY):
        at = LOW * CY * core + r
        mine_ref[r] = field_ref[pl.ds(at, WIN, stride=CY), :]
        at = LOW * CY * (1 - core) + r
        mate_ref[r * WIN : (r + 1) * WIN, :] = field_ref[pl.ds(at, WIN, stride=CY), :]
    base = CY * WIN
    rows = [cell_ref[...].astype(jnp.float32)] + [corner_ref[n] for n in range(4)]
    table = jnp.concatenate(rows + [jnp.zeros((3, slots), jnp.float32)], axis=0)
    table_ref[...] = table
    for part in range(slots // COLS):
        mate_ref[base + 8 * part : base + 8 * part + 8, :] = table[:, part * COLS : (part + 1) * COLS]


def route(own_ref, inv_ref, inno_ref, out_ref, pad_ref):
    count = own_ref.shape[1]
    tiles = out_ref.shape[0] // (2 * CAP)
    chips = tiles // 2
    own = own_ref[...]
    owners = lax.broadcasted_iota(jnp.int32, (tiles, count), 0)
    onehot = jnp.where(owners == own, 1.0, 0.0)
    at = lax.broadcasted_iota(jnp.int32, (count, count), 0)
    to = lax.broadcasted_iota(jnp.int32, (count, count), 1)
    before = jnp.where(at < to, 1.0, 0.0).astype(jnp.bfloat16)
    earlier = dot(onehot.astype(jnp.bfloat16), before, ((1,), (0,)))
    rank = jnp.sum(onehot * earlier, axis=0, keepdims=True)
    chip_here = lax.broadcasted_iota(jnp.int32, (chips, count), 0) == (own >> 1)
    even = (own & 1) == 0
    picks = []
    for r in range(CAP):
        hit = jnp.where(chip_here & (rank == float(r)), 1.0, 0.0)
        picks.append(jnp.concatenate([jnp.where(even, hit, 0.0), jnp.where(even, 0.0, hit)], axis=1))
    pick = jnp.concatenate(picks, axis=0).astype(jnp.bfloat16)
    inv = inv_ref[...]
    pad_ref[...] = jnp.zeros_like(pad_ref)
    pad_ref[0:CHAN, :] = inv
    pad_ref[FULL : FULL + CHAN, :] = inv * inno_ref[...]
    zero = jnp.zeros((2 * WIN, count), jnp.float32)
    for core in range(2):
        at = LOW * core
        both = jnp.concatenate([pad_ref[at : at + WIN, :], pad_ref[FULL + at : FULL + at + WIN, :]], axis=0)
        block = jnp.concatenate(
            [jnp.concatenate([both, zero], axis=1), jnp.concatenate([zero, both], axis=1)], axis=0
        )
        first, rest = block.astype(jnp.bfloat16), block
        rest = rest - first.astype(jnp.float32)
        second, third = split(rest)
        total = dot(pick, first, ((1,), (1,)))
        total = total + dot(pick, second, ((1,), (1,)))
        total = total + dot(pick, third, ((1,), (1,)))
        for r in range(CAP):
            part = total[r * chips : (r + 1) * chips]
            edge = jnp.zeros((1, COLS), jnp.float32)
            below = jnp.concatenate([edge, part[: chips - 1]], axis=0)
            above = jnp.concatenate([part[1:], edge], axis=0)
            lane = lax.broadcasted_iota(jnp.int32, (chips, COLS), 1)
            low = jnp.where(lane < WIN, pltpu.roll(below, COLS - WIN, 1), pltpu.roll(below, 2 * WIN, 1))
            high = jnp.where(lane < 3 * WIN, pltpu.roll(above, WIN, 1), above)
            at = 2 * core * CAP + r
            out_ref[pl.ds(at, chips, stride=4 * CAP), :] = part
            out_ref[pl.ds(at + CAP, chips, stride=4 * CAP), :] = jnp.where(lane < 2 * WIN, low, high)


def spread_out(misfit, high_ref, low_ref):
    high, low = split(misfit)
    wide = dot(jnp.concatenate([high, low], axis=0), high_ref[...], ((1,), (1,)))
    return wide[:WIN] + wide[WIN:] + dot(high, low_ref[...], ((1,), (1,)))


def adjoint(misfits, high_ref, low_ref, store):
    for tile in range(2):
        flat = spread_out(misfits[tile], high_ref.at[tile], low_ref.at[tile])
        for r in range(CY):
            store(tile * CY + r, flat[:, r * COLS : (r + 1) * COLS])


def fill(table, rows, high_ref, low_ref):
    columns = lax.broadcasted_iota(jnp.int32, (COLS, table.shape[1]), 0)
    cell = table[0:1].astype(jnp.int32)
    row = jnp.zeros_like(cell)
    for edge in range(1, CY - 1):
        row = row + jnp.where(cell >= edge * (COLS - 1), 1, 0)
    col = cell - row * (COLS - 1)
    at_col, at_next = col == columns, col + 1 == columns
    for n, r in enumerate(rows):
        lower, upper = row == r, row == r - 1
        west = jnp.where(lower, table[1:2], 0.0) + jnp.where(upper, table[3:4], 0.0)
        east = jnp.where(lower, table[2:3], 0.0) + jnp.where(upper, table[4:5], 0.0)
        matrix = jnp.where(at_col, west, 0.0) + jnp.where(at_next, east, 0.0)
        high, low = split(matrix)
        high_ref[n * COLS : (n + 1) * COLS, :] = high
        low_ref[n * COLS : (n + 1) * COLS, :] = low


def chip_body(core_ref, mine_ref, theirs_ref, table_ref, d_ref, tables_ref, up_ref, down_ref):
    core = core_ref[0]
    slots = table_ref.shape[1]
    parts = slots // COLS
    base = CY * WIN
    other = jnp.concatenate([theirs_ref[base + 8 * n : base + 8 * n + 8, :] for n in range(parts)], axis=1)
    here = table_ref[...]
    up_ref[FAR] = jnp.zeros((WIN, COLS), jnp.float32)
    for tile in range(2):
        first = core == tile
        table = jnp.where(first, here, other)
        tables_ref[tile] = table
        for r in range(CY):
            d_ref[tile * CY + r] = jnp.where(first, mine_ref[r], theirs_ref[r * WIN : (r + 1) * WIN, :])
        for n in range(parts):
            at = (tile * parts + n) * 8
            up_ref[FAR, at : at + 8, :] = table[:, n * COLS : (n + 1) * COLS]
    up_ref[0:FAR] = d_ref[0:FAR]
    down_ref[0:FAR] = d_ref[ROWS - FAR : ROWS]
    down_ref[FAR] = up_ref[FAR]


def seed_body(d_ref, tables_ref, south_d, north_d, rec_ref, *outs):
    high_ref, low_ref, weight_ref, g_ref, south_ref, north_ref, slot_ref, beside_high, beside_low = outs
    count = rec_ref.shape[0] // (2 * CAP)
    parts = slot_ref.shape[0] // COLS

    def received(half):
        for r in range(CAP):
            at = half * CAP + r
            slot_ref[pl.ds(r, count, stride=CAP), :] = rec_ref[pl.ds(at, count, stride=2 * CAP), :]
        return slot_ref[...].T

    slot_t = received(0)
    targets = []
    for tile in range(2):
        fill(tables_ref[tile], range(CY), high_ref.at[tile], low_ref.at[tile])
        weight_ref[tile] = slot_t[tile * 2 * WIN : tile * 2 * WIN + WIN]
        targets.append(slot_t[tile * 2 * WIN + WIN : (tile + 1) * 2 * WIN])

    def store(row, value):
        g_ref[row] = jnp.sqrt(d_ref[row]) * value

    adjoint(targets, high_ref, low_ref, store)
    beside = received(1)
    for n, (halo_d, out_ref) in enumerate(((south_d, south_ref), (north_d, north_ref))):
        out_ref[FAR : 2 * FAR] = halo_d[0:FAR]
        for tile in range(2):
            whole = tile == 1 - n
            rows = range(CY) if whole else (range(2 * CY - FAR, CY) if n == 0 else range(FAR - CY))
            at = (0, FAR - CY)[tile] if n == 0 else (0, CY)[tile]
            table = jnp.concatenate(
                [halo_d[FAR, (tile * parts + m) * 8 : (tile * parts + m + 1) * 8, :] for m in range(parts)], axis=1
            )
            size = len(rows) * COLS
            fill(table, rows, beside_high, beside_low)
            target = beside[(2 * n + tile) * WIN : (2 * n + tile + 1) * WIN]
            flat = spread_out(target, beside_high.at[0:size], beside_low.at[0:size])
            for m in range(len(rows)):
                out_ref[at + m] = jnp.sqrt(halo_d[at + m]) * flat[:, m * COLS : (m + 1) * COLS]


def places(halo):
    each = COLS // halo
    rows = range(1, ROWS + 2 * halo - 1)
    return [(row, n // each, n % each) for n, row in enumerate(rows)], -(-len(rows) // each)


def strips_body(halo, kinds, *refs):
    heres, (south_ref, north_ref, west_ref, east_ref) = refs[:kinds], refs[kinds:]
    spots, tiles = places(halo)
    lane = lax.broadcasted_iota(jnp.int32, (WIN, COLS), 1)
    for kind in range(kinds):
        for tile in range(tiles):
            west = jnp.zeros((WIN, COLS), jnp.float32)
            east = jnp.zeros((WIN, COLS), jnp.float32)
            for row, own_tile, q in spots:
                if own_tile != tile:
                    continue
                if row < halo:
                    line = south_ref[kind * halo + row]
                elif row < halo + ROWS:
                    line = heres[kind][row - halo]
                else:
                    line = north_ref[kind * halo + row - halo - ROWS]
                inside = (lane >= halo * q) & (lane < halo * q + halo)
                west = jnp.where(inside, pltpu.roll(line, halo * q, 1) if q else line, west)
                east = jnp.where(inside, pltpu.roll(line, (halo * q + halo) % COLS, 1), east)
            west_ref[kind * tiles + tile] = west
            east_ref[kind * tiles + tile] = east


def extend(dst, halo, offset, kind, here_ref, south_ref, north_ref, east_ref, west_ref):
    spots, tiles = places(halo)
    where_of = {row: (tile, q) for row, tile, q in spots}
    lane = lax.broadcasted_iota(jnp.int32, (WIN, COLS), 1)
    for row in range(ROWS + 2 * halo):
        if row < halo:
            line = south_ref[kind * halo + row]
        elif row < halo + ROWS:
            line = here_ref[row - halo]
        else:
            line = north_ref[kind * halo + row - halo - ROWS]
        dst[offset + row, :, 0:COLS] = line
        beyond = jnp.zeros((WIN, COLS), jnp.float32)
        if row in where_of:
            tile, q = where_of[row]
            right, left = east_ref[kind * tiles + tile], west_ref[kind * tiles + tile]
            right = pltpu.roll(right, COLS - halo * q, 1) if q else right
            left = pltpu.roll(left, COLS - halo - halo * q, 1)
            beyond = jnp.where(lane < halo, right, jnp.where(lane >= COLS - halo, left, 0.0))
        dst[offset + row, :, COLS:] = beyond


def sweep(src, dst, d_ref, low, high):
    lane = lax.broadcasted_iota(jnp.int32, (WIN, COLS), 1)
    last, first = lane == COLS - 1, lane == 0

    def body(row, carry):
        before, now = carry
        after = src[row + 1]
        a, b = now[:, :COLS], now[:, COLS:]
        east_a, east_b = pltpu.roll(a, COLS - 1, 1), pltpu.roll(b, COLS - 1, 1)
        west_a, west_b = pltpu.roll(a, 1, 1), pltpu.roll(b, 1, 1)
        beside_a = jnp.where(last, east_b, east_a) + jnp.where(first, west_b, west_a)
        beside_b = jnp.where(last, east_a, east_b) + jnp.where(first, west_a, west_b)
        beside = jnp.concatenate([beside_a, beside_b], axis=1)
        dst[row] = now + d_ref[row] * (before + after + beside - 4.0 * now)
        return now, after

    carry = (src[low - 1], src[low])
    for row in range(low, high):
        carry = body(row, carry)


def unscale(value, d):
    return jnp.where(d > 0.0, value * lax.rsqrt(jnp.where(d > 0.0, d, 1.0)), 0.0)


def largest(value):
    top = jnp.max(jnp.max(jnp.abs(value), axis=1, keepdims=True), axis=0, keepdims=True)
    return jnp.maximum(top, 1e-30)


def whole_sum(value):
    return jnp.sum(jnp.sum(value, axis=1, keepdims=True), axis=0, keepdims=True)


def pair_body(later, *refs):
    refs = list(refs)
    core_ref = refs.pop(0)
    here_ref, south_ref, north_ref, east_ref, west_ref = refs[:5]
    refs = refs[5:]
    if later:
        wide_d, high_ref, low_ref, weight_ref, q_in, u_in = refs[:6]
        q_ref, up_ref, down_ref, g_ref, stats_ref, first_ref, second_ref = refs[6:]
    else:
        d_ref, high_ref, low_ref, weight_ref = refs[:4]
        q_ref, u_ref, wide_d, up_ref, down_ref, g_ref, first_ref, second_ref = refs[4:]
        extend(wide_d, FAR, 0, 1, d_ref, south_ref, north_ref, east_ref, west_ref)
    extend(first_ref, FAR, 0, 0, here_ref, south_ref, north_ref, east_ref, west_ref)
    src, dst = first_ref, second_ref
    total = ROWS + 2 * FAR
    halo = STEPS if later else FAR
    rows = []
    for step in range(1, FAR + 1):
        sweep(src, dst, wide_d, step, total - step)
        src, dst = dst, src
        if step == STEPS:
            for r in range(ROWS):
                value = unscale(src[FAR + r, :, 0:COLS], wide_d[FAR + r, :, 0:COLS])
                q_ref[r] = q_in[r] + value if later else value
    for r in range(ROWS):
        value = unscale(src[FAR + r, :, 0:COLS], wide_d[FAR + r, :, 0:COLS])
        if later:
            value = value + u_in[r]
        else:
            u_ref[r] = value
        rows.append(value)
    misfits, samples = [], []
    for tile in range(2):
        flat = jnp.concatenate(rows[tile * CY : (tile + 1) * CY], axis=1)
        high, low = split(flat)
        both = dot(jnp.concatenate([high, low], axis=0), high_ref[tile], ((1,), (0,)))
        value = both[:WIN] + both[WIN:] + dot(high, low_ref[tile], ((1,), (0,)))
        samples.append(value)
        misfits.append(weight_ref[tile] * value)

    def store(row, value):
        g_ref[row] = jnp.sqrt(wide_d[FAR + row, :, 0:COLS]) * value

    adjoint(misfits, high_ref, low_ref, store)
    up_ref[...] = g_ref[0:halo]
    down_ref[...] = g_ref[ROWS - halo : ROWS]
    if later:
        sub = lax.broadcasted_iota(jnp.int32, (WIN, 1), 0)
        keep = jnp.where((sub < LOW) | (core_ref[0] == 1), 1.0, 0.0)
        top0 = jnp.zeros((WIN, COLS), jnp.float32)
        top1 = jnp.zeros((WIN, COLS), jnp.float32)
        for r in range(ROWS):
            top0 = jnp.maximum(top0, jnp.abs(q_in[r]))
            top1 = jnp.maximum(top1, jnp.abs(q_ref[r]))
        t0, t1 = largest(top0), largest(top1)
        v1 = jnp.maximum(largest(samples[0]), largest(samples[1]))
        i0, i1, iv = 1.0 / t0, 1.0 / t1, 1.0 / v1
        sums = [jnp.zeros((WIN, COLS), jnp.float32) for _ in range(3)]
        for r in range(ROWS):
            a, b = q_in[r] * i0, q_ref[r] * i1
            sums = [sums[0] + a * a, sums[1] + a * b, sums[2] + b * b]
        values = [whole_sum(s * keep) for s in sums]
        quad = sum(weight_ref[tile] * (samples[tile] * iv) * (samples[tile] * iv) for tile in range(2))
        values += [whole_sum(quad * keep), t0, t1, v1]
        stats_ref[...] = jnp.broadcast_to(as_row(values), stats_ref.shape)


def as_row(values):
    lane = lax.broadcasted_iota(jnp.int32, (1, COLS), 1)
    row = jnp.zeros((1, COLS), jnp.float32)
    for n, value in enumerate(values):
        row = jnp.where(lane == n, value, row)
    return row


def merged(block):
    part = [block[:, n : n + 1] for n in range(7)]
    tops = [jnp.max(part[n], axis=0, keepdims=True) for n in (4, 5, 6)]
    r0, r1, rv = (part[4 + n] / tops[n] for n in range(3))
    values = [part[0] * r0 * r0, part[1] * r0 * r1, part[2] * r1 * r1, part[3] * rv * rv]
    return [jnp.sum(value, axis=0, keepdims=True) for value in values] + tops


def merge_body(in_ref, out_ref):
    out_ref[...] = jnp.broadcast_to(as_row(merged(in_ref[...]))[None], out_ref.shape)


def last_body(core_ref, here_ref, south_ref, north_ref, east_ref, west_ref, wide_d, q0_ref, q1_ref, *outs):
    mine_ref, mate_ref, first_ref, second_ref, near_d, q2_ref = outs
    core = core_ref[0]
    total = ROWS + 2 * STEPS
    extend(first_ref, STEPS, 0, 0, here_ref, south_ref, north_ref, east_ref, west_ref)
    for row in range(total):
        near_d[row] = wide_d[row + FAR - STEPS]
    src, dst = first_ref, second_ref
    for step in range(1, STEPS + 1):
        sweep(src, dst, near_d, step, total - step)
        src, dst = dst, src
    for r in range(ROWS):
        d = near_d[STEPS + r, :, 0:COLS]
        q2_ref[r] = q1_ref[r] + unscale(src[STEPS + r, :, 0:COLS], d)
    for n, q in enumerate((q0_ref, q1_ref, q2_ref)):
        mine_ref[n * CY : (n + 1) * CY] = q[pl.ds(core * CY, CY)]
        mate_ref[n * CY : (n + 1) * CY] = q[pl.ds((1 - core) * CY, CY)]


def final_body(core_ref, mine_ref, theirs_ref, stats_ref, control_ref, residual_ref, c_ref, r_ref):
    core = core_ref[0]
    m00, m01, m11, s11, t0, t1, v1 = merged(stats_ref[:, 0, :])
    ratio = t1 / t0
    scaled = m00 / m01
    alpha0 = scaled / ratio
    norm1 = m00 - 2.0 * scaled * m01 + scaled * scaled * m11
    beta = norm1 / m00
    lift = 1.0 + beta
    relative = v1 / t1
    curve = lift * lift * ratio * m01 - 2.0 * lift * scaled * ratio * m11
    curve = curve + scaled * scaled * (m11 + relative * relative * s11)
    alpha1 = norm1 / curve
    one = alpha0 + alpha1 * lift
    two = alpha1 * alpha0
    for ref, owner in ((mine_ref, core), (theirs_ref, 1 - core)):
        for r in range(CY):
            q0, q1, q2 = ref[r], ref[CY + r], ref[2 * CY + r]
            at = LOW * CY * owner + r
            c_ref[pl.ds(at, WIN, stride=CY), :] = one * q0 - two * q1
            r_ref[pl.ds(at, WIN, stride=CY), :] = q0 - one * q1 + two * q2
    control_ref[...] = c_ref[0 : CHAN * CY, :].reshape(CHAN, CY, COLS)
    residual_ref[...] = r_ref[0 : CHAN * CY, :].reshape(CHAN, CY, COLS)


def on_device(
    diffusivity, land_mask, innovation, inverse_variance, owner_ids, cell_index, corner_weights
):
    count_x, count_y = lax.axis_size("gx"), lax.axis_size("gy")
    slots = count_y * CAP
    core = (lax.axis_index("gy") % 2).astype(jnp.int32).reshape(1)
    count = owner_ids.shape[0]

    def along_y(value, by):
        pairs = [(i, i + by) for i in range(count_y) if 0 <= i + by < count_y]
        return lax.ppermute(value, "gy", pairs)

    def along_x(value, by):
        return lax.ppermute(value, "gx", [(i, (i + by) % count_x) for i in range(count_x)])

    def across(value):
        return lax.ppermute(value, "gy", [(i, i ^ 1) for i in range(count_y)])

    def exchange(heres, up, down, halo):
        return sideways(heres, along_y(down, 2), along_y(up, -2), halo)

    def sideways(heres, south, north, halo):
        kinds = len(heres)
        tiles = places(halo)[1]
        pack = call(functools.partial(strips_body, halo, kinds), [f32(kinds * tiles, WIN, COLS)] * 2, 10**6)
        west, east = pack(*heres, south, north)
        return south, north, along_x(west, -1), along_x(east, 1)

    field = f32(ROWS, WIN, COLS)
    ins = [
        owner_ids.reshape(1, count), inverse_variance, innovation, diffusivity, land_mask, cell_index, corner_weights
    ]
    space = [pltpu.VMEM(x.shape, x.dtype) for x in ins]
    space += [pltpu.VMEM((2 * FULL, count), jnp.float32), pltpu.VMEM((FULL * CY, COLS), jnp.float32)]
    chunks, mine, mate, table = call(
        first_body,
        [f32(2 * slots, COLS), f32(CY, WIN, COLS), f32(CY * WIN + 8 * (slots // COLS), COLS), f32(8, slots)],
        10**7,
        space + [pltpu.SemaphoreType.DMA((len(ins),))],
        1,
        pltpu.HBM,
    )(core, *(pltpu.with_memory_space_constraint(x, pltpu.HBM) for x in ins))
    theirs = across(mate)
    received = lax.all_to_all(chunks, "gy", split_axis=0, concat_axis=0, tiled=True)
    matrix = jax.ShapeDtypeStruct((2, CY * COLS, slots), jnp.bfloat16)
    sent = f32(FAR + 1, WIN, COLS)
    d, tables, up, down = call(chip_body, [field, f32(2, 8, slots), sent, sent], 10**6, (), 1)(
        core, mine, theirs, table
    )
    both = f32(2 * FAR, WIN, COLS)
    space = [pltpu.VMEM((slots, COLS), jnp.float32)] + [pltpu.VMEM((CY * COLS, slots), jnp.bfloat16)] * 2
    outs = [matrix, matrix, f32(2, WIN, slots), field, both, both]
    high, low, weights, g, south, north = call(seed_body, outs, 10**8, space)(
        d, tables, along_y(down, 2), along_y(up, -2), received
    )
    wide = (ROWS + 2 * FAR, WIN, 2 * COLS)
    space = [pltpu.VMEM(wide, jnp.float32)] * 2
    south, north, east, west = sideways([g, d], south, north, FAR)
    q0, u0, wide_d, up, down, g = call(
        functools.partial(pair_body, False),
        [field, field, f32(*wide), f32(FAR, WIN, COLS), f32(FAR, WIN, COLS), field],
        2 * 10**8,
        space,
        1,
    )(core, g, south, north, east, west, d, high, low, weights)
    south, north, east, west = exchange([g], up, down, FAR)
    q1, up, down, g, stats = call(
        functools.partial(pair_body, True),
        [field, f32(STEPS, WIN, COLS), f32(STEPS, WIN, COLS), field, f32(count_y, COLS)],
        2 * 10**8,
        space,
        1,
    )(core, g, south, north, east, west, wide_d, high, low, weights, q0, u0)
    stats = lax.all_to_all(stats, "gy", split_axis=0, concat_axis=0, tiled=True)
    (stats,) = call(merge_body, [f32(count_x, 1, COLS)], 10**5)(stats)
    south, north, east, west = exchange([g], up, down, STEPS)
    stats = lax.all_to_all(stats, "gx", split_axis=0, concat_axis=0, tiled=True)
    near = (ROWS + 2 * STEPS, WIN, 2 * COLS)
    mine, mate = call(
        last_body,
        [f32(3 * CY, WIN, COLS)] * 2,
        10**8,
        [pltpu.VMEM(near, jnp.float32)] * 3 + [pltpu.VMEM((ROWS, WIN, COLS), jnp.float32)],
        1,
    )(core, g, south, north, east, west, wide_d, q0, q1)
    mate, stats = lax.optimization_barrier((mate, stats))
    theirs = across(mate)
    out = f32(CHAN, CY, COLS)
    return call(
        final_body, [out, out], 10**6, [pltpu.VMEM((FULL * CY, COLS), jnp.float32)] * 2, 1
    )(core, mine, theirs, stats)


def solution(mesh):
    return jax.shard_map(
        on_device,
        mesh=mesh,
        in_specs=(
            P(None, "gy", "gx"),
            P("gy", "gx"),
            P(None, ("gx", "gy")),
            P(None, ("gx", "gy")),
            P(("gx", "gy"), None),
            P(("gx", "gy"), None),
            P(None, ("gx", "gy"), None),
        ),
        out_specs=(P(None, "gy", "gx"), P(None, "gy", "gx")),
        check_vma=False,
    )
```

```python
import functools

import jax
import jax.numpy as jnp
from jax import lax
from jax.experimental import pallas as pl
from jax.experimental.pallas import tpu as pltpu
from jax.sharding import PartitionSpec as P

CAP = 4
STEPS = 5
CHAN = 50
WIN = 32
LOW = 24
FULL = 56
COLS = 128
CY = 8
ROWS = 2 * CY
FAR = 2 * STEPS


def call(body, outs, flops, scratch=(), scalars=0, source=pltpu.VMEM):
    def run(*args):
        size = sum(a.size * a.dtype.itemsize for a in args) + sum(o.size * o.dtype.itemsize for o in outs)
        specs = [pl.BlockSpec(memory_space=pltpu.SMEM)] * scalars
        specs += [pl.BlockSpec(memory_space=source)] * (len(args) - scalars)
        return pl.pallas_call(
            body,
            out_shape=tuple(outs),
            in_specs=specs,
            out_specs=tuple(pl.BlockSpec(memory_space=pltpu.VMEM) for _ in outs),
            scratch_shapes=list(scratch),
            compiler_params=pltpu.CompilerParams(vmem_limit_bytes=16 * 1024 * 1024),
            cost_estimate=pl.CostEstimate(flops=flops, bytes_accessed=size, transcendentals=0),
        )(*args)

    return run


def f32(*shape):
    return jax.ShapeDtypeStruct(shape, jnp.float32)


def split(value):
    high = value.astype(jnp.bfloat16)
    return high, (value - high.astype(jnp.float32)).astype(jnp.bfloat16)


def dot(a, b, dims):
    return lax.dot_general(a, b, (dims, ((), ())), preferred_element_type=jnp.float32)


def first_body(core_ref, *refs):
    ins, (chunk_ref, mine_ref, mate_ref, table_ref), space = refs[:7], refs[7:11], refs[11:]
    held, pad_ref, field_ref, sems = space[:7], space[7], space[8], space[9]
    copies = [pltpu.make_async_copy(ins[n], held[n], sems.at[n]) for n in range(7)]
    for copy in copies:
        copy.start()
    own_ref, inv_ref, inno_ref, diff_ref, mask_ref, cell_ref, corner_ref = held
    for copy in copies:
        copy.wait()
    route(own_ref, inv_ref, inno_ref, chunk_ref, pad_ref)
    core = core_ref[0]
    slots = cell_ref.shape[1]
    masked = diff_ref[...] * mask_ref[...].astype(jnp.float32)[None]
    field_ref[0 : CHAN * CY, :] = masked.reshape(CHAN * CY, COLS)
    field_ref[CHAN * CY :, :] = jnp.zeros((FULL * CY - CHAN * CY, COLS), jnp.float32)
    for r in range(CY):
        at = LOW * CY * core + r
        mine_ref[r] = field_ref[pl.ds(at, WIN, stride=CY), :]
        at = LOW * CY * (1 - core) + r
        mate_ref[r * WIN : (r + 1) * WIN, :] = field_ref[pl.ds(at, WIN, stride=CY), :]
    base = CY * WIN
    rows = [cell_ref[...].astype(jnp.float32)] + [corner_ref[n] for n in range(4)]
    table = jnp.concatenate(rows + [jnp.zeros((3, slots), jnp.float32)], axis=0)
    table_ref[...] = table
    for part in range(slots // COLS):
        mate_ref[base + 8 * part : base + 8 * part + 8, :] = table[:, part * COLS : (part + 1) * COLS]


def route(own_ref, inv_ref, inno_ref, out_ref, pad_ref):
    count = own_ref.shape[1]
    tiles = out_ref.shape[0] // (2 * CAP)
    chips = tiles // 2
    own = own_ref[...]
    owners = lax.broadcasted_iota(jnp.int32, (tiles, count), 0)
    onehot = jnp.where(owners == own, 1.0, 0.0)
    at = lax.broadcasted_iota(jnp.int32, (count, count), 0)
    to = lax.broadcasted_iota(jnp.int32, (count, count), 1)
    before = jnp.where(at < to, 1.0, 0.0).astype(jnp.bfloat16)
    earlier = dot(onehot.astype(jnp.bfloat16), before, ((1,), (0,)))
    rank = jnp.sum(onehot * earlier, axis=0, keepdims=True)
    chip_here = lax.broadcasted_iota(jnp.int32, (chips, count), 0) == (own >> 1)
    even = (own & 1) == 0
    picks = []
    for r in range(CAP):
        hit = jnp.where(chip_here & (rank == float(r)), 1.0, 0.0)
        picks.append(jnp.concatenate([jnp.where(even, hit, 0.0), jnp.where(even, 0.0, hit)], axis=1))
    pick = jnp.concatenate(picks, axis=0).astype(jnp.bfloat16)
    inv = inv_ref[...]
    pad_ref[...] = jnp.zeros_like(pad_ref)
    pad_ref[0:CHAN, :] = inv
    pad_ref[FULL : FULL + CHAN, :] = inv * inno_ref[...]
    zero = jnp.zeros((2 * WIN, count), jnp.float32)
    for core in range(2):
        at = LOW * core
        both = jnp.concatenate([pad_ref[at : at + WIN, :], pad_ref[FULL + at : FULL + at + WIN, :]], axis=0)
        block = jnp.concatenate(
            [jnp.concatenate([both, zero], axis=1), jnp.concatenate([zero, both], axis=1)], axis=0
        )
        first, rest = block.astype(jnp.bfloat16), block
        rest = rest - first.astype(jnp.float32)
        second, third = split(rest)
        total = dot(pick, first, ((1,), (1,)))
        total = total + dot(pick, second, ((1,), (1,)))
        total = total + dot(pick, third, ((1,), (1,)))
        for r in range(CAP):
            part = total[r * chips : (r + 1) * chips]
            edge = jnp.zeros((1, COLS), jnp.float32)
            below = jnp.concatenate([edge, part[: chips - 1]], axis=0)
            above = jnp.concatenate([part[1:], edge], axis=0)
            lane = lax.broadcasted_iota(jnp.int32, (chips, COLS), 1)
            low = jnp.where(lane < WIN, pltpu.roll(below, COLS - WIN, 1), pltpu.roll(below, 2 * WIN, 1))
            high = jnp.where(lane < 3 * WIN, pltpu.roll(above, WIN, 1), above)
            at = 2 * core * CAP + r
            out_ref[pl.ds(at, chips, stride=4 * CAP), :] = part
            out_ref[pl.ds(at + CAP, chips, stride=4 * CAP), :] = jnp.where(lane < 2 * WIN, low, high)


def spread_out(misfit, high_ref, low_ref):
    high, low = split(misfit)
    wide = dot(jnp.concatenate([high, low], axis=0), high_ref[...], ((1,), (1,)))
    return wide[:WIN] + wide[WIN:] + dot(high, low_ref[...], ((1,), (1,)))


def adjoint(misfits, high_ref, low_ref, store):
    for tile in range(2):
        flat = spread_out(misfits[tile], high_ref.at[tile], low_ref.at[tile])
        for r in range(CY):
            store(tile * CY + r, flat[:, r * COLS : (r + 1) * COLS])


def fill(table, rows, high_ref, low_ref):
    columns = lax.broadcasted_iota(jnp.int32, (COLS, table.shape[1]), 0)
    cell = table[0:1].astype(jnp.int32)
    row = jnp.zeros_like(cell)
    for edge in range(1, CY - 1):
        row = row + jnp.where(cell >= edge * (COLS - 1), 1, 0)
    col = cell - row * (COLS - 1)
    at_col, at_next = col == columns, col + 1 == columns
    for n, r in enumerate(rows):
        lower, upper = row == r, row == r - 1
        west = jnp.where(lower, table[1:2], 0.0) + jnp.where(upper, table[3:4], 0.0)
        east = jnp.where(lower, table[2:3], 0.0) + jnp.where(upper, table[4:5], 0.0)
        matrix = jnp.where(at_col, west, 0.0) + jnp.where(at_next, east, 0.0)
        high, low = split(matrix)
        high_ref[n * COLS : (n + 1) * COLS, :] = high
        low_ref[n * COLS : (n + 1) * COLS, :] = low


def chip_body(core_ref, mine_ref, theirs_ref, table_ref, d_ref, tables_ref, up_ref, down_ref):
    core = core_ref[0]
    slots = table_ref.shape[1]
    parts = slots // COLS
    base = CY * WIN
    other = jnp.concatenate([theirs_ref[base + 8 * n : base + 8 * n + 8, :] for n in range(parts)], axis=1)
    here = table_ref[...]
    up_ref[FAR] = jnp.zeros((WIN, COLS), jnp.float32)
    for tile in range(2):
        first = core == tile
        table = jnp.where(first, here, other)
        tables_ref[tile] = table
        for r in range(CY):
            d_ref[tile * CY + r] = jnp.where(first, mine_ref[r], theirs_ref[r * WIN : (r + 1) * WIN, :])
        for n in range(parts):
            at = (tile * parts + n) * 8
            up_ref[FAR, at : at + 8, :] = table[:, n * COLS : (n + 1) * COLS]
    up_ref[0:FAR] = d_ref[0:FAR]
    down_ref[0:FAR] = d_ref[ROWS - FAR : ROWS]
    down_ref[FAR] = up_ref[FAR]


def seed_body(d_ref, tables_ref, south_d, north_d, rec_ref, *outs):
    high_ref, low_ref, weight_ref, g_ref, south_ref, north_ref, slot_ref, beside_high, beside_low = outs
    count = rec_ref.shape[0] // (2 * CAP)
    parts = slot_ref.shape[0] // COLS

    def received(half):
        for r in range(CAP):
            at = half * CAP + r
            slot_ref[pl.ds(r, count, stride=CAP), :] = rec_ref[pl.ds(at, count, stride=2 * CAP), :]
        return slot_ref[...].T

    slot_t = received(0)
    targets = []
    for tile in range(2):
        fill(tables_ref[tile], range(CY), high_ref.at[tile], low_ref.at[tile])
        weight_ref[tile] = slot_t[tile * 2 * WIN : tile * 2 * WIN + WIN]
        targets.append(slot_t[tile * 2 * WIN + WIN : (tile + 1) * 2 * WIN])

    def store(row, value):
        g_ref[row] = jnp.sqrt(d_ref[row]) * value

    adjoint(targets, high_ref, low_ref, store)
    beside = received(1)
    for n, (halo_d, out_ref) in enumerate(((south_d, south_ref), (north_d, north_ref))):
        out_ref[FAR : 2 * FAR] = halo_d[0:FAR]
        for tile in range(2):
            whole = tile == 1 - n
            rows = range(CY) if whole else (range(2 * CY - FAR, CY) if n == 0 else range(FAR - CY))
            at = (0, FAR - CY)[tile] if n == 0 else (0, CY)[tile]
            table = jnp.concatenate(
                [halo_d[FAR, (tile * parts + m) * 8 : (tile * parts + m + 1) * 8, :] for m in range(parts)], axis=1
            )
            size = len(rows) * COLS
            fill(table, rows, beside_high, beside_low)
            target = beside[(2 * n + tile) * WIN : (2 * n + tile + 1) * WIN]
            flat = spread_out(target, beside_high.at[0:size], beside_low.at[0:size])
            for m in range(len(rows)):
                out_ref[at + m] = jnp.sqrt(halo_d[at + m]) * flat[:, m * COLS : (m + 1) * COLS]


def places(halo):
    each = COLS // halo
    rows = range(1, ROWS + 2 * halo - 1)
    return [(row, n // each, n % each) for n, row in enumerate(rows)], -(-len(rows) // each)


def strips_body(halo, kinds, *refs):
    heres, (south_ref, north_ref, west_ref, east_ref) = refs[:kinds], refs[kinds:]
    spots, tiles = places(halo)
    lane = lax.broadcasted_iota(jnp.int32, (WIN, COLS), 1)
    for kind in range(kinds):
        for tile in range(tiles):
            west = jnp.zeros((WIN, COLS), jnp.float32)
            east = jnp.zeros((WIN, COLS), jnp.float32)
            for row, own_tile, q in spots:
                if own_tile != tile:
                    continue
                if row < halo:
                    line = south_ref[kind * halo + row]
                elif row < halo + ROWS:
                    line = heres[kind][row - halo]
                else:
                    line = north_ref[kind * halo + row - halo - ROWS]
                inside = (lane >= halo * q) & (lane < halo * q + halo)
                west = jnp.where(inside, pltpu.roll(line, halo * q, 1) if q else line, west)
                east = jnp.where(inside, pltpu.roll(line, (halo * q + halo) % COLS, 1), east)
            west_ref[kind * tiles + tile] = west
            east_ref[kind * tiles + tile] = east


def extend(dst, halo, offset, kind, here_ref, south_ref, north_ref, east_ref, west_ref):
    spots, tiles = places(halo)
    where_of = {row: (tile, q) for row, tile, q in spots}
    lane = lax.broadcasted_iota(jnp.int32, (WIN, COLS), 1)
    for row in range(ROWS + 2 * halo):
        if row < halo:
            line = south_ref[kind * halo + row]
        elif row < halo + ROWS:
            line = here_ref[row - halo]
        else:
            line = north_ref[kind * halo + row - halo - ROWS]
        dst[offset + row, :, 0:COLS] = line
        beyond = jnp.zeros((WIN, COLS), jnp.float32)
        if row in where_of:
            tile, q = where_of[row]
            right, left = east_ref[kind * tiles + tile], west_ref[kind * tiles + tile]
            right = pltpu.roll(right, COLS - halo * q, 1) if q else right
            left = pltpu.roll(left, COLS - halo - halo * q, 1)
            beyond = jnp.where(lane < halo, right, jnp.where(lane >= COLS - halo, left, 0.0))
        dst[offset + row, :, COLS:] = beyond


def sweep(src, dst, d_ref, low, high):
    at = lax.broadcasted_iota(jnp.int32, (COLS, 2 * COLS), 0)
    to = lax.broadcasted_iota(jnp.int32, (COLS, 2 * COLS), 1)
    near = (jnp.abs(at - to) == 1) & (to < COLS)
    cross = ((at == 0) & (to == 2 * COLS - 1)) | ((at == COLS - 1) & (to == COLS))
    shift = jnp.where(near | cross, 1.0, 0.0).astype(jnp.bfloat16)
    lane = lax.broadcasted_iota(jnp.int32, (WIN, COLS), 1)
    last, first = lane == COLS - 1, lane == 0
    before, now = src[low - 1], src[low]
    for row in range(low, high):
        after = src[row + 1]
        a, b = now[:, :COLS], now[:, COLS:]
        x, y = split(a)
        both = dot(jnp.concatenate([x, y], axis=0), shift, ((1,), (0,)))
        both = both[:WIN] + both[WIN:]
        e, w = pltpu.roll(b, COLS - 1, 1), pltpu.roll(b, 1, 1)
        beside_a = both[:, :COLS] + jnp.where(last, e, jnp.where(first, w, 0.0))
        beside_b = both[:, COLS:] + jnp.where(last, 0.0, e) + jnp.where(first, 0.0, w)
        beside = jnp.concatenate([beside_a, beside_b], axis=1)
        dst[row] = now + d_ref[row] * (before + after + beside - 4.0 * now)
        before, now = now, after


def unscale(value, d):
    return jnp.where(d > 0.0, value * lax.rsqrt(jnp.where(d > 0.0, d, 1.0)), 0.0)


def largest(value):
    top = jnp.max(jnp.max(jnp.abs(value), axis=1, keepdims=True), axis=0, keepdims=True)
    return jnp.maximum(top, 1e-30)


def whole_sum(value):
    return jnp.sum(jnp.sum(value, axis=1, keepdims=True), axis=0, keepdims=True)


def pair_body(later, *refs):
    refs = list(refs)
    core_ref = refs.pop(0)
    here_ref, south_ref, north_ref, east_ref, west_ref = refs[:5]
    refs = refs[5:]
    if later:
        wide_d, high_ref, low_ref, weight_ref, q_in, u_in = refs[:6]
        q_ref, up_ref, down_ref, g_ref, stats_ref, first_ref, second_ref = refs[6:]
    else:
        d_ref, high_ref, low_ref, weight_ref = refs[:4]
        q_ref, u_ref, wide_d, up_ref, down_ref, g_ref, first_ref, second_ref = refs[4:]
        extend(wide_d, FAR, 0, 1, d_ref, south_ref, north_ref, east_ref, west_ref)
    extend(first_ref, FAR, 0, 0, here_ref, south_ref, north_ref, east_ref, west_ref)
    src, dst = first_ref, second_ref
    total = ROWS + 2 * FAR
    halo = STEPS if later else FAR
    rows = []
    for step in range(1, FAR + 1):
        sweep(src, dst, wide_d, step, total - step)
        src, dst = dst, src
        if step == STEPS:
            for r in range(ROWS):
                value = unscale(src[FAR + r, :, 0:COLS], wide_d[FAR + r, :, 0:COLS])
                q_ref[r] = q_in[r] + value if later else value
    for r in range(ROWS):
        value = unscale(src[FAR + r, :, 0:COLS], wide_d[FAR + r, :, 0:COLS])
        if later:
            value = value + u_in[r]
        else:
            u_ref[r] = value
        rows.append(value)
    misfits, samples = [], []
    for tile in range(2):
        flat = jnp.concatenate(rows[tile * CY : (tile + 1) * CY], axis=1)
        high, low = split(flat)
        both = dot(jnp.concatenate([high, low], axis=0), high_ref[tile], ((1,), (0,)))
        value = both[:WIN] + both[WIN:] + dot(high, low_ref[tile], ((1,), (0,)))
        samples.append(value)
        misfits.append(weight_ref[tile] * value)

    def store(row, value):
        g_ref[row] = jnp.sqrt(wide_d[FAR + row, :, 0:COLS]) * value

    adjoint(misfits, high_ref, low_ref, store)
    up_ref[...] = g_ref[0:halo]
    down_ref[...] = g_ref[ROWS - halo : ROWS]
    if later:
        sub = lax.broadcasted_iota(jnp.int32, (WIN, 1), 0)
        keep = jnp.where((sub < LOW) | (core_ref[0] == 1), 1.0, 0.0)
        top0 = jnp.zeros((WIN, COLS), jnp.float32)
        top1 = jnp.zeros((WIN, COLS), jnp.float32)
        for r in range(ROWS):
            top0 = jnp.maximum(top0, jnp.abs(q_in[r]))
            top1 = jnp.maximum(top1, jnp.abs(q_ref[r]))
        t0, t1 = largest(top0), largest(top1)
        v1 = jnp.maximum(largest(samples[0]), largest(samples[1]))
        i0, i1, iv = 1.0 / t0, 1.0 / t1, 1.0 / v1
        sums = [jnp.zeros((WIN, COLS), jnp.float32) for _ in range(3)]
        for r in range(ROWS):
            a, b = q_in[r] * i0, q_ref[r] * i1
            sums = [sums[0] + a * a, sums[1] + a * b, sums[2] + b * b]
        values = [whole_sum(s * keep) for s in sums]
        quad = sum(weight_ref[tile] * (samples[tile] * iv) * (samples[tile] * iv) for tile in range(2))
        values += [whole_sum(quad * keep), t0, t1, v1]
        stats_ref[...] = jnp.broadcast_to(as_row(values), stats_ref.shape)


def as_row(values):
    lane = lax.broadcasted_iota(jnp.int32, (1, COLS), 1)
    row = jnp.zeros((1, COLS), jnp.float32)
    for n, value in enumerate(values):
        row = jnp.where(lane == n, value, row)
    return row


def merged(block):
    part = [block[:, n : n + 1] for n in range(7)]
    tops = [jnp.max(part[n], axis=0, keepdims=True) for n in (4, 5, 6)]
    r0, r1, rv = (part[4 + n] / tops[n] for n in range(3))
    values = [part[0] * r0 * r0, part[1] * r0 * r1, part[2] * r1 * r1, part[3] * rv * rv]
    return [jnp.sum(value, axis=0, keepdims=True) for value in values] + tops


def merge_body(in_ref, out_ref):
    out_ref[...] = jnp.broadcast_to(as_row(merged(in_ref[...]))[None], out_ref.shape)


def last_body(core_ref, here_ref, south_ref, north_ref, east_ref, west_ref, wide_d, q0_ref, q1_ref, *outs):
    mine_ref, mate_ref, first_ref, second_ref, near_d, q2_ref = outs
    core = core_ref[0]
    total = ROWS + 2 * STEPS
    extend(first_ref, STEPS, 0, 0, here_ref, south_ref, north_ref, east_ref, west_ref)
    for row in range(total):
        near_d[row] = wide_d[row + FAR - STEPS]
    src, dst = first_ref, second_ref
    for step in range(1, STEPS + 1):
        sweep(src, dst, near_d, step, total - step)
        src, dst = dst, src
    for r in range(ROWS):
        d = near_d[STEPS + r, :, 0:COLS]
        q2_ref[r] = q1_ref[r] + unscale(src[STEPS + r, :, 0:COLS], d)
    for n, q in enumerate((q0_ref, q1_ref, q2_ref)):
        mine_ref[n * CY : (n + 1) * CY] = q[pl.ds(core * CY, CY)]
        mate_ref[n * CY : (n + 1) * CY] = q[pl.ds((1 - core) * CY, CY)]


def final_body(core_ref, mine_ref, theirs_ref, stats_ref, control_ref, residual_ref, c_ref, r_ref):
    core = core_ref[0]
    m00, m01, m11, s11, t0, t1, v1 = merged(stats_ref[:, 0, :])
    ratio = t1 / t0
    scaled = m00 / m01
    alpha0 = scaled / ratio
    norm1 = m00 - 2.0 * scaled * m01 + scaled * scaled * m11
    beta = norm1 / m00
    lift = 1.0 + beta
    relative = v1 / t1
    curve = lift * lift * ratio * m01 - 2.0 * lift * scaled * ratio * m11
    curve = curve + scaled * scaled * (m11 + relative * relative * s11)
    alpha1 = norm1 / curve
    one = alpha0 + alpha1 * lift
    two = alpha1 * alpha0
    for ref, owner in ((mine_ref, core), (theirs_ref, 1 - core)):
        for r in range(CY):
            q0, q1, q2 = ref[r], ref[CY + r], ref[2 * CY + r]
            at = LOW * CY * owner + r
            c_ref[pl.ds(at, WIN, stride=CY), :] = one * q0 - two * q1
            r_ref[pl.ds(at, WIN, stride=CY), :] = q0 - one * q1 + two * q2
    control_ref[...] = c_ref[0 : CHAN * CY, :].reshape(CHAN, CY, COLS)
    residual_ref[...] = r_ref[0 : CHAN * CY, :].reshape(CHAN, CY, COLS)


def on_device(
    diffusivity, land_mask, innovation, inverse_variance, owner_ids, cell_index, corner_weights
):
    count_x, count_y = lax.axis_size("gx"), lax.axis_size("gy")
    slots = count_y * CAP
    core = (lax.axis_index("gy") % 2).astype(jnp.int32).reshape(1)
    count = owner_ids.shape[0]

    def along_y(value, by):
        pairs = [(i, i + by) for i in range(count_y) if 0 <= i + by < count_y]
        return lax.ppermute(value, "gy", pairs)

    def along_x(value, by):
        return lax.ppermute(value, "gx", [(i, (i + by) % count_x) for i in range(count_x)])

    def across(value):
        return lax.ppermute(value, "gy", [(i, i ^ 1) for i in range(count_y)])

    def exchange(heres, up, down, halo):
        return sideways(heres, along_y(down, 2), along_y(up, -2), halo)

    def sideways(heres, south, north, halo):
        kinds = len(heres)
        tiles = places(halo)[1]
        pack = call(functools.partial(strips_body, halo, kinds), [f32(kinds * tiles, WIN, COLS)] * 2, 10**6)
        west, east = pack(*heres, south, north)
        return south, north, along_x(west, -1), along_x(east, 1)

    field = f32(ROWS, WIN, COLS)
    ins = [
        owner_ids.reshape(1, count), inverse_variance, innovation, diffusivity, land_mask, cell_index, corner_weights
    ]
    space = [pltpu.VMEM(x.shape, x.dtype) for x in ins]
    space += [pltpu.VMEM((2 * FULL, count), jnp.float32), pltpu.VMEM((FULL * CY, COLS), jnp.float32)]
    chunks, mine, mate, table = call(
        first_body,
        [f32(2 * slots, COLS), f32(CY, WIN, COLS), f32(CY * WIN + 8 * (slots // COLS), COLS), f32(8, slots)],
        10**7,
        space + [pltpu.SemaphoreType.DMA((len(ins),))],
        1,
        pltpu.HBM,
    )(core, *(pltpu.with_memory_space_constraint(x, pltpu.HBM) for x in ins))
    theirs = across(mate)
    received = lax.all_to_all(chunks, "gy", split_axis=0, concat_axis=0, tiled=True)
    matrix = jax.ShapeDtypeStruct((2, CY * COLS, slots), jnp.bfloat16)
    sent = f32(FAR + 1, WIN, COLS)
    d, tables, up, down = call(chip_body, [field, f32(2, 8, slots), sent, sent], 10**6, (), 1)(
        core, mine, theirs, table
    )
    both = f32(2 * FAR, WIN, COLS)
    space = [pltpu.VMEM((slots, COLS), jnp.float32)] + [pltpu.VMEM((CY * COLS, slots), jnp.bfloat16)] * 2
    outs = [matrix, matrix, f32(2, WIN, slots), field, both, both]
    high, low, weights, g, south, north = call(seed_body, outs, 10**8, space)(
        d, tables, along_y(down, 2), along_y(up, -2), received
    )
    wide = (ROWS + 2 * FAR, WIN, 2 * COLS)
    space = [pltpu.VMEM(wide, jnp.float32)] * 2
    south, north, east, west = sideways([g, d], south, north, FAR)
    q0, u0, wide_d, up, down, g = call(
        functools.partial(pair_body, False),
        [field, field, f32(*wide), f32(FAR, WIN, COLS), f32(FAR, WIN, COLS), field],
        2 * 10**8,
        space,
        1,
    )(core, g, south, north, east, west, d, high, low, weights)
    south, north, east, west = exchange([g], up, down, FAR)
    q1, up, down, g, stats = call(
        functools.partial(pair_body, True),
        [field, f32(STEPS, WIN, COLS), f32(STEPS, WIN, COLS), field, f32(count_y, COLS)],
        2 * 10**8,
        space,
        1,
    )(core, g, south, north, east, west, wide_d, high, low, weights, q0, u0)
    stats = lax.all_to_all(stats, "gy", split_axis=0, concat_axis=0, tiled=True)
    (stats,) = call(merge_body, [f32(count_x, 1, COLS)], 10**5)(stats)
    south, north, east, west = exchange([g], up, down, STEPS)
    stats = lax.all_to_all(stats, "gx", split_axis=0, concat_axis=0, tiled=True)
    near = (ROWS + 2 * STEPS, WIN, 2 * COLS)
    mine, mate = call(
        last_body,
        [f32(3 * CY, WIN, COLS)] * 2,
        10**8,
        [pltpu.VMEM(near, jnp.float32)] * 3 + [pltpu.VMEM((ROWS, WIN, COLS), jnp.float32)],
        1,
    )(core, g, south, north, east, west, wide_d, q0, q1)
    mate, stats = lax.optimization_barrier((mate, stats))
    theirs = across(mate)
    out = f32(CHAN, CY, COLS)
    return call(
        final_body, [out, out], 10**6, [pltpu.VMEM((FULL * CY, COLS), jnp.float32)] * 2, 1
    )(core, mine, theirs, stats)


def solution(mesh):
    return jax.shard_map(
        on_device,
        mesh=mesh,
        in_specs=(
            P(None, "gy", "gx"),
            P("gy", "gx"),
            P(None, ("gx", "gy")),
            P(None, ("gx", "gy")),
            P(("gx", "gy"), None),
            P(("gx", "gy"), None),
            P(None, ("gx", "gy"), None),
        ),
        out_specs=(P(None, "gy", "gx"), P(None, "gy", "gx")),
        check_vma=False,
    )
```
